512 devices in a mesh: segment: 16 (over y, x_hi, core), dp: 32 (over z, x_lo).
Axes of the slice: x: 4 (x_hi: 2, x_lo: 2; x = x_hi * 2 + x_lo), y: 4, z: 16, core: 2. Of those that a mesh axis runs over, the one named last changes fastest.
Arguments:
- hidden_in: bfloat16 [8, 512, 9216], P(None, 'dp', 'segment'), may hold values from -6 to 6
- cotangent: bfloat16 [8, 512, 9216], P(None, 'dp', 'segment'), may hold values from -0.25 to 0.25
- stored_bases: bfloat16 [16, 8, 512, 9216], P('segment', None, 'dp'), may hold values from -6 to 6
- sample_ids: int32 [32, 8], P('dp'), may hold values from 0 to 7, each once within a row
- block_exps: int32 [16, 8, 512, 72], P('segment', None, 'dp'), may hold values from -9 to -4
- ln_gains: bfloat16 [16, 9216], P('segment'), may hold values from 0.099609375 to 1.8984375
- w_down: bfloat16 [16, 9216, 16], P('segment'), may hold values from -0.0625 to 0.0625
- w_up: bfloat16 [16, 16, 9216], P('segment'), may hold values from -0.375 to 0.375
Outputs:
- grad_down: bfloat16 [16, 9216, 16], P('segment')
- grad_up: bfloat16 [16, 16, 9216], P('segment')
The draws below stay inside these ranges and needn't reach their ends.
Inputs may be any that keep to these rules, and one draw needn't show every extreme that they name: Each row of sample_ids names every slot 0 to 7 once.
All inputs are finite; a program needn't handle non-finite values.
Results may differ from the reference program's by a relative error of at most 0.04.
Values may be sent and summed in bfloat16 or wider, within the bound.
A program may use at most 128 MiB of HBM per device.

```python
import jax
import jax.numpy as jnp
from jax import lax

D = 9216
R = 16
M = 8
TOK_DEV = 16
NB = 72
TOKENS = 512
N_SEGMENT = 16
N_DP = 32


def set_ends(values, stream_key, low, high):
    dims = values.shape
    place = [jax.random.randint(jax.random.fold_in(stream_key, axis), (), 0, dims[axis]) for axis in range(len(dims))]
    values = values.at[tuple(place)].set(low)
    longest = dims.index(max(dims))
    place[longest] = (place[longest] + 1) % dims[longest]
    return values.at[tuple(place)].set(high)


def block_levels(key, extent, split, least, largest):
    factor_of, own = 1.0, jax.random.fold_in(key, 6)
    for dim, shards_of in split:
        draws = jnp.exp(jax.random.uniform(jax.random.fold_in(own, dim), (shards_of,), jnp.float32, least / len(split), largest / len(split)))
        factor_of = factor_of * jnp.repeat(draws, extent[dim] // shards_of).reshape([-1 if axis == dim else 1 for axis in range(len(extent))])
    return factor_of


def bell_draw(stream_key, extent, scale, bound, split=(), kind=jnp.bfloat16):
    loudness = block_levels(stream_key, extent, split, -0.22, 0.18) if split else 1.0
    array = jax.random.normal(stream_key, extent, jnp.float32) * scale * loudness
    return jnp.minimum(jnp.maximum(array, -bound), bound).astype(kind)


def setup_inputs(seed: int = 0) -> dict:
    key_list = jax.random.split(jax.random.key(seed), 9)
    return {
        "hidden_in": bell_draw(key_list[0], (M, TOKENS, D), 1.0, 6.0, ((1, 32), (2, 16))),
        "cotangent": bell_draw(key_list[1], (M, TOKENS, D), (1.0 / (M * TOKENS) ** 0.5), 0.25, ((1, 32), (2, 16))),
        "stored_bases": bell_draw(key_list[2], (N_SEGMENT, M, TOKENS, D), 1.0, 6.0, ((0, 16), (2, 32))),
        "sample_ids": jax.vmap(lambda own: jax.random.permutation(own, M))(jax.random.split(key_list[3], N_DP)).reshape((N_DP, M)).astype(jnp.int32),
        "block_exps": set_ends(jax.random.randint(key_list[4], (N_SEGMENT, M, TOKENS, NB), -9, -3), jax.random.fold_in(key_list[4], 1), -9, (-3) - 1).astype(jnp.int32),
        "ln_gains": jnp.clip(1.0 + 0.18 * jax.random.normal(key_list[5], (N_SEGMENT, D), jnp.float32), 0.099609375, 1.8984375).astype(jnp.bfloat16),
        "w_down": bell_draw(key_list[6], (N_SEGMENT, D, R), D ** -0.5, 0.0625, ((0, 16),)),
        "w_up": bell_draw(key_list[7], (N_SEGMENT, R, D), (16 * R) ** -0.5, 0.375, ((0, 16),)),
    }


def block_factor(exp_rows):
    magnitude = -exp_rows
    factor = jnp.ones(exp_rows.shape, jnp.float32)
    for bit_pos in range(5):
        factor = jnp.where((magnitude >> bit_pos) % 2 == 1, factor * jnp.float32(0.5 ** (1 << bit_pos)), factor)
    return factor

def layer_norm(values, scales):
    center = values - lax.optimization_barrier(jnp.mean(values, axis=-1, keepdims=True))
    spread = lax.optimization_barrier(jnp.mean(center * center, axis=-1, keepdims=True))
    return center * lax.rsqrt(spread + 1e-05) * scales

def decode_input(arrived, base_rows, exp_rows):
    row_count = arrived.shape[0]
    blocks = exp_rows.shape[1]
    factor = block_factor(exp_rows)[:, :, None]
    delta_rows = (arrived.astype(jnp.float32) - base_rows.astype(jnp.float32)).reshape(row_count, blocks, -1)
    scaled = (delta_rows / factor).astype(jnp.bfloat16)
    scaled = lax.optimization_barrier(scaled).astype(jnp.float32)
    clipped = jnp.clip(scaled, -448.0, 448.0)
    return base_rows.astype(jnp.float32) + (clipped * factor).reshape(row_count, -1)

def gelu_tanh(pre_act):
    return jax.nn.gelu(pre_act, approximate=True)

def section_forward(arrived, base_rows, exp_rows, scales, down_proj, up_proj):
    decoded = decode_input(arrived, base_rows, exp_rows)
    normed = layer_norm(decoded, scales).astype(jnp.bfloat16)
    before = jnp.dot(normed, down_proj, preferred_element_type=jnp.float32)
    activated = gelu_tanh(before).astype(jnp.bfloat16)
    output = (decoded + jnp.dot(activated, up_proj, preferred_element_type=jnp.float32)).astype(jnp.bfloat16)
    return (output, (decoded, normed, before, activated))

def section_backward(grad_out, saved_parts, scales, down_proj, up_proj):
    decoded, normed, before, activated = saved_parts
    grad_upward = jnp.dot(activated.T, grad_out, preferred_element_type=jnp.float32)
    grad_activated = jnp.dot(grad_out, up_proj.T, preferred_element_type=jnp.float32)
    _, gelu_pull = jax.vjp(gelu_tanh, before)
    grad_before = gelu_pull(grad_activated)[0].astype(jnp.bfloat16)
    grad_downward = jnp.dot(normed.T, grad_before, preferred_element_type=jnp.float32)
    grad_normed = jnp.dot(grad_before, down_proj.T, preferred_element_type=jnp.float32)
    _, norm_pull = jax.vjp(lambda inner_rows: layer_norm(inner_rows, scales), decoded)
    grad_decoded = grad_out.astype(jnp.float32) + norm_pull(grad_normed)[0]
    grad_in = grad_decoded.astype(jnp.bfloat16)
    return (grad_in, grad_downward, grad_upward)

def reference(hidden_in, cotangent, stored_bases, sample_ids, block_exps, ln_gains, w_down, w_up):

    def replica(replica_pos):
        row_start = replica_pos * TOK_DEV
        first_rows = lax.dynamic_slice_in_dim(hidden_in, row_start, TOK_DEV, 1).reshape(M * TOK_DEV, D)
        last_grad = lax.dynamic_slice_in_dim(cotangent, row_start, TOK_DEV, 1).reshape(M * TOK_DEV, D)
        bases_here = lax.dynamic_slice_in_dim(stored_bases, row_start, TOK_DEV, 2)
        exps_here = lax.dynamic_slice_in_dim(block_exps, row_start, TOK_DEV, 2).reshape(N_SEGMENT, M * TOK_DEV, NB)
        slot_ids = lax.dynamic_index_in_dim(sample_ids, replica_pos, 0, keepdims=False).astype(jnp.int32)
        chosen = jnp.take(bases_here, slot_ids, axis=1).reshape(N_SEGMENT, M * TOK_DEV, D)
        arrived = first_rows
        kept_inputs = []
        for section in range(N_SEGMENT):
            kept_inputs.append(arrived)
            arrived, _ = section_forward(arrived, chosen[section], exps_here[section], ln_gains[section].astype(jnp.float32), w_down[section], w_up[section])
        grad_out = last_grad
        downs = [None] * N_SEGMENT
        ups = [None] * N_SEGMENT
        for section in reversed(range(N_SEGMENT)):
            scales = ln_gains[section].astype(jnp.float32)
            _, saved_parts = section_forward(kept_inputs[section], chosen[section], exps_here[section], scales, w_down[section], w_up[section])
            grad_out, part_down, part_up = section_backward(grad_out, saved_parts, scales, w_down[section], w_up[section])
            downs[section] = part_down.astype(jnp.bfloat16)
            ups[section] = part_up.astype(jnp.bfloat16)
        return (jnp.stack(downs), jnp.stack(ups))
    replica_downs, replica_ups = lax.map(replica, jnp.arange(N_DP, dtype=jnp.int32))
    grad_down = lax.optimization_barrier(jnp.sum(replica_downs.astype(jnp.float32), axis=0)).astype(jnp.bfloat16)
    grad_up = lax.optimization_barrier(jnp.sum(replica_ups.astype(jnp.float32), axis=0)).astype(jnp.bfloat16)
    return (grad_down, grad_up)
```

```python
import functools

import jax
import jax.numpy as jnp
from jax import lax
from jax.experimental import pallas as pl
from jax.experimental.pallas import tpu as pltpu
from jax.sharding import PartitionSpec as P

MESH = pl.DeviceIdType.MESH
F32 = jnp.float32
BF16 = jnp.bfloat16
NSEC = 16
UNITS = 16
NCH = 8
CH = 1152
WIDTH = NCH * CH
PART = 576
NZ = 16
ROWS = 64
AHEAD = 16
NT = (((1,), (1,)), ((), ()))
TN = (((0,), (0,)), ((), ()))
K_GELU = 0.7978845608028654
C_GELU = 0.044715


def dot(a, b, dims=(((1,), (0,)), ((), ()))):
    return lax.dot_general(a, b, dims, preferred_element_type=F32)


def lanes(shape):
    return lax.broadcasted_iota(jnp.int32, shape, len(shape) - 1)


def gelu(x):
    return 0.5 * x * (1.0 + jnp.tanh(K_GELU * (x + C_GELU * x * x * x)))


def gelu_slope(x):
    th = jnp.tanh(K_GELU * (x + C_GELU * x * x * x))
    return 0.5 * (1.0 + th) + 0.5 * x * (1.0 - th * th) * K_GELU * (1.0 + 3.0 * C_GELU * x * x)


def power_of_two(exps):
    factor = jnp.ones(exps.shape, F32)
    for bit in range(5):
        factor = jnp.where(((-exps) >> bit) & 1 == 1, factor * F32(0.5 ** (1 << bit)), factor)
    return factor


def join_parts(ref):
    first = ref[0].reshape(ROWS, 640).astype(F32)
    second = ref[1].reshape(ROWS, 640).astype(F32)
    lane = lanes((ROWS, 128))
    turned = [pltpu.roll(second[:, 128 * i : 128 * i + 128], 64, 1) for i in range(5)]
    tiles = [first[:, 128 * i : 128 * i + 128] for i in range(4)]
    tiles.append(jnp.where(lane < 64, first[:, 512:640], turned[0]))
    for i in range(4):
        tiles.append(jnp.where(lane < 64, turned[i], turned[i + 1]))
    return jnp.concatenate(tiles, axis=1)


def sections_kernel(
    ids_ref, hid_ref, cot_ref, store_ref, exps_ref, gains_ref, wd_ref, wu_ref,
    parts_ref,
    hid_s, cot_s, fac_s, wts_s, aux_s,
    hid_r, cot_r, fac_r, wts_r, aux_r, base_r,
    spread, wu_all, wuc_all, wdc_all, a_ref, g_ref, d_ref, pay, bpad, bef_all, bef_ref, act_ref,
    mean_ref, rstd_ref, xhat_ref,
    stat_s, stat_r, mix_s, mix_r, cw_s, cw_r, gm_ref, xt_ref, gb_s, gb_r,
    sem_hs, sem_hr, sem_cs, sem_cr, sem_data_s, sem_fac, sem_wts, sem_aux, sem_base,
    sem_st_s, sem_st_r, sem_mx_s, sem_mx_r, sem_cw_s, sem_cw_r, sem_gb_s, sem_gb_r,
):
    me = lax.axis_index("segment")
    dp = lax.axis_index("dp")
    y, xh, core = me // 4, (me // 2) % 2, me % 2
    chunk = 2 * y + core

    def seg_of_chunk(q):
        return 4 * (q // 2) + 2 * xh + q % 2

    barrier = pltpu.get_barrier_semaphore()

    def greet(j, _):
        pl.semaphore_signal(
            barrier, inc=1, device_id=(lax.rem(me + j, NSEC), dp), device_id_type=MESH
        )
        return 0

    lax.fori_loop(1, NSEC, greet, 0)

    hid_s[...] = jnp.zeros(hid_s.shape, BF16)
    cot_s[...] = jnp.zeros(cot_s.shape, BF16)
    fac_s[...] = jnp.zeros(fac_s.shape, BF16)
    for slot in range(8):
        batch = jnp.int32(0)
        for k in range(8):
            batch = jnp.maximum(batch, jnp.where(ids_ref[0, k] == slot, k, 0))
        hid_s[slot, :, 0:PART] = hid_ref[batch]
        cot_s[slot, :, 0:PART] = cot_ref[batch]
        fac_s[slot, :, 0:72] = power_of_two(exps_ref[batch]).astype(BF16)
    lane16 = lanes((UNITS, 128))
    aux = jnp.zeros((UNITS, 128), F32)
    up_total = jnp.zeros((UNITS, 1), F32)
    down_total = jnp.zeros((UNITS, 1), F32)
    for q in range(NCH):
        part = slice(q * CH, (q + 1) * CH)
        scaled = (wd_ref[:, part].astype(F32) * gains_ref[:, part].astype(F32)).astype(BF16)
        wts_s[0:UNITS, part] = scaled
        up = wu_ref[:, part]
        wts_s[UNITS : 2 * UNITS, part] = up
        down_sum = jnp.sum(scaled.astype(F32), axis=1, keepdims=True)
        aux = aux + jnp.where(lane16 == 16 + q, down_sum, 0.0)
        down_total = down_total + down_sum
        up_total = up_total + jnp.sum(up.astype(F32), axis=1, keepdims=True)
    aux = aux + jnp.where(lane16 == 0, down_total * (1.0 / WIDTH), 0.0)
    aux_s[...] = aux + jnp.where(lane16 == 1, up_total * (1.0 / WIDTH), 0.0)

    pl.semaphore_wait(barrier, NSEC - 1)

    def part_copy(x_to, src, dst, send, recv, go):
        target = 4 * y + 2 * x_to + xh
        rows = src.at[4 * x_to : 4 * x_to + 4]

        if go:

            @pl.when(target == me)
            def _():
                pltpu.make_async_copy(rows, dst.at[core], recv.at[core]).start()

        @pl.when(target != me)
        def _():
            copy = pltpu.make_async_remote_copy(
                src_ref=rows, dst_ref=dst.at[core], send_sem=send.at[x_to],
                recv_sem=recv.at[core], device_id=(target, dp), device_id_type=MESH,
            )
            copy.start() if go else copy.wait_send()

    for x_to in range(2):
        part_copy(x_to, hid_s, hid_r, sem_hs, sem_hr, True)

    def data_copies(j):
        target = lax.rem(me + j, NSEC)
        to_chunk = 2 * (target // 4) + target % 2
        slots = pl.ds(4 * ((target // 2) % 2), 4)
        cols = pl.ds(pl.multiple_of(to_chunk * CH, 128), CH)
        pairs = (
            (fac_s.at[slots], fac_r.at[me], sem_fac),
            (aux_s, aux_r.at[me], sem_aux),
            (wts_s.at[:, cols], wts_r.at[me], sem_wts),
            (store_ref.at[slots, :, cols], base_r.at[me], sem_base),
        )
        return [
            pltpu.make_async_remote_copy(
                src_ref=src, dst_ref=dst, send_sem=sem_data_s.at[i, j], recv_sem=sem.at[me],
                device_id=(target, dp), device_id_type=MESH,
            )
            for i, (src, dst, sem) in enumerate(pairs)
        ]

    def send_section():
        slots = pl.ds(4 * xh, 4)
        cols = pl.ds(pl.multiple_of(chunk * CH, 128), CH)
        for src, dst, sem in (
            (fac_s.at[slots], fac_r.at[me], sem_fac),
            (aux_s, aux_r.at[me], sem_aux),
            (wts_s.at[:, cols], wts_r.at[me], sem_wts),
            (store_ref.at[slots, :, cols], base_r.at[me], sem_base),
        ):
            pltpu.make_async_copy(src, dst, sem.at[me]).start()

        def one(j, _):
            for copy in data_copies(j):
                copy.start()
            return 0

        lax.fori_loop(1, NSEC, one, 0)

    @pl.when(me < AHEAD)
    def _():
        send_section()

    for x_to in range(2):
        part_copy(x_to, cot_s, cot_r, sem_cs, sem_cr, True)

    block = lax.broadcasted_iota(jnp.int32, (128, CH), 0)
    feature = lax.broadcasted_iota(jnp.int32, (128, CH), 1)
    spread[...] = jnp.where(block == 9 * chunk + feature // 128, 1.0, 0.0).astype(BF16)
    pay[...] = jnp.zeros(pay.shape, F32)
    bpad[...] = jnp.zeros(bpad.shape, F32)
    bef_all[...] = jnp.zeros(bef_all.shape, F32)
    wuc_all[...] = jnp.zeros(wuc_all.shape, BF16)

    for h in range(2):
        pltpu.make_async_copy(hid_r.at[h], hid_r.at[h], sem_hr.at[h]).wait()
    a_ref[...] = join_parts(hid_r)

    lane = lanes((ROWS, 128))

    def stat_copy(s, j):
        target = seg_of_chunk(lax.rem(chunk + j, NCH))
        return pltpu.make_async_remote_copy(
            src_ref=stat_s.at[s], dst_ref=stat_r.at[s, j - 1], send_sem=sem_st_s.at[s, j - 1],
            recv_sem=sem_st_r.at[s, j - 1], device_id=(target, dp), device_id_type=MESH,
        )

    def mix_copy(s, j):
        to_chunk = lax.rem(chunk + j, NCH)
        return pltpu.make_async_remote_copy(
            src_ref=mix_s.at[s, to_chunk], dst_ref=mix_r.at[s, j - 1],
            send_sem=sem_mx_s.at[s, j - 1], recv_sem=sem_mx_r.at[s, j - 1],
            device_id=(seg_of_chunk(to_chunk), dp), device_id_type=MESH,
        )

    def side_work(s):
        xhat = ((d_ref[...] - mean_ref[s]) * rstd_ref[s]).astype(BF16)
        xhat_ref[s] = xhat
        ups = wuc_all[...]
        rows = dot(xhat, ups, NT)
        gram = dot(wdc_all[s], ups, NT)
        for q in range(NCH):
            mix_s[s, q, 0:8] = rows[8 * q : 8 * q + 8]
            mix_s[s, q, 8:24] = gram
        for j in range(1, NCH):
            mix_copy(s, j).start()
        bpad[:, 0:UNITS] = bef_ref[s]
        bef_all[s // 8] = bef_all[s // 8] + pltpu.roll(bpad[...], 16 * (s % 8), 1)

    def step(s, _):
        @pl.when(me == s + AHEAD)
        def _():
            send_section()

        for ref, sem in ((fac_r, sem_fac), (aux_r, sem_aux), (wts_r, sem_wts), (base_r, sem_base)):
            pltpu.make_async_copy(ref.at[s], ref.at[s], sem.at[s]).wait()
        small = fac_r[s].reshape(ROWS, 128)
        wide = small.astype(F32)
        inverse = jnp.where(wide > 0.0, 1.0 / jnp.where(wide > 0.0, wide, 1.0), 0.0).astype(BF16)
        factor = dot(small, spread[...])
        scale = dot(inverse, spread[...])
        base = base_r[s].reshape(ROWS, CH).astype(F32)
        coded = ((a_ref[...] - base) * scale).astype(BF16).astype(F32)
        decoded = base + jnp.clip(coded, -448.0, 448.0) * factor
        own_mean = jnp.sum(decoded, axis=1, keepdims=True) * (1.0 / CH)
        center = decoded - own_mean
        own_m2 = jnp.sum(center * center, axis=1, keepdims=True)
        pay[:, 0:UNITS] = dot(center.astype(BF16), wts_r[s, 0:UNITS, :], NT)
        row = jnp.where(lane == 16 + chunk, own_mean, pay[...])
        row = jnp.where(lane == 24, own_m2, row)
        packed = row[0:16]
        for g in range(1, 4):
            packed = packed + pltpu.roll(row[16 * g : 16 * g + 16], 32 * g, 1)
        stat_s[s] = packed
        for j in range(1, NCH):
            stat_copy(s, j).start()

        @pl.when(s > 0)
        def _():
            side_work(s - 1)

        d_ref[...] = decoded
        up = wts_r[s, UNITS : 2 * UNITS, :]
        wu_all[pl.ds(pl.multiple_of(s * UNITS, UNITS), UNITS), :] = up
        wuc_all[pl.ds(pl.multiple_of(s * UNITS, UNITS), UNITS), :] = (
            up.astype(F32) - aux_r[s, :, 1:2]
        ).astype(BF16)
        wdc_all[s] = (wts_r[s, 0:UNITS, :].astype(F32) - aux_r[s, :, 0:1]).astype(BF16)

        for j in range(1, NCH):
            stat_copy(s, j).wait_recv()
        total = stat_s[s]
        for j in range(NCH - 1):
            total = total + stat_r[s, j]
        rows = jnp.concatenate(
            [total] + [pltpu.roll(total, 128 - 32 * g, 1) for g in range(1, 4)], axis=0
        )
        is_mean = (lane >= 16) & (lane < 24)
        mean = jnp.sum(jnp.where(is_mean, rows, 0.0), axis=1, keepdims=True) * (1.0 / NCH)
        off = jnp.where(is_mean, rows - mean, 0.0)
        spread_sum = jnp.sum(
            jnp.where(lane == 24, rows, 0.0) + CH * off * off, axis=1, keepdims=True
        )
        rstd = lax.rsqrt(spread_sum * (1.0 / WIDTH) + 1e-05)
        shift = dot(off.astype(BF16), aux_r[s].astype(BF16), NT)
        before = (rows[:, 0:UNITS] + shift) * rstd
        act = gelu(before).astype(BF16)
        a_ref[...] = (decoded + dot(act, up)).astype(BF16).astype(F32)
        bef_ref[s] = before
        act_ref[s] = act
        mean_ref[s] = mean
        rstd_ref[s] = rstd
        return 0

    lax.fori_loop(0, NSEC, step, 0)
    side_work(NSEC - 1)

    for h in range(2):
        pltpu.make_async_copy(cot_r.at[h], cot_r.at[h], sem_cr.at[h]).wait()
    cot = join_parts(cot_r)
    g_ref[...] = cot
    cw_s[...] = dot(cot.astype(BF16), wu_all[...], NT)

    def cw_copy(j):
        to_chunk = lax.rem(chunk + j, NCH)
        return pltpu.make_async_remote_copy(
            src_ref=cw_s.at[pl.ds(pl.multiple_of(8 * to_chunk, 8), 8)], dst_ref=cw_r.at[j - 1],
            send_sem=sem_cw_s.at[j - 1], recv_sem=sem_cw_r.at[j - 1],
            device_id=(seg_of_chunk(to_chunk), dp), device_id_type=MESH,
        )

    for j in range(1, NCH):
        cw_copy(j).start()

    mine = pl.ds(pl.multiple_of(8 * chunk, 8), 8)

    def fold(t, _):
        for j in range(1, NCH):
            mix_copy(t, j).wait_recv()
        both = mix_s[t, chunk]
        for j in range(NCH - 1):
            both = both + mix_r[t, j]
        both = jnp.where(lanes((24, 256)) < UNITS * t, both, 0.0)
        xt_ref[t] = both[0:8]
        gm_ref[pl.ds(pl.multiple_of(t * UNITS, UNITS), UNITS), :] = both[8:24].astype(BF16)
        return 0

    lax.fori_loop(0, NSEC, fold, 0)
    bef8 = jnp.concatenate([bef_all[0, mine, :], bef_all[1, mine, :]], axis=1)
    slope8 = gelu_slope(bef8)
    lane8 = lanes((8, 256))
    for j in range(1, NCH):
        cw_copy(j).wait_recv()
    grad_act = cw_s[mine, :]
    for j in range(NCH - 1):
        grad_act = grad_act + cw_r[j]

    def back(i, carry):
        grad_act, out = carry
        t = NSEC - 1 - i
        here = (lane8 >= UNITS * t) & (lane8 < UNITS * t + UNITS)
        grad_bef = jnp.where(here, grad_act * slope8, 0.0).astype(BF16)
        wide = grad_bef.astype(F32)
        c2 = jnp.sum(wide * bef8, axis=1, keepdims=True) * (1.0 / WIDTH)
        change = dot(grad_bef, gm_ref[...]) - c2 * xt_ref[t]
        return grad_act + rstd_ref[t, mine, :] * change, out + wide

    _, grad_bef = lax.fori_loop(0, NSEC, back, (grad_act, jnp.zeros((8, 256), F32)))
    gb_s[0] = grad_bef[:, 0:128]
    gb_s[1] = grad_bef[:, 128:256]

    def gb_copy(j):
        target = seg_of_chunk(lax.rem(chunk + j, NCH))
        return pltpu.make_async_remote_copy(
            src_ref=gb_s, dst_ref=gb_r.at[:, mine], send_sem=sem_gb_s.at[j - 1],
            recv_sem=sem_gb_r.at[j - 1], device_id=(target, dp), device_id_type=MESH,
        )

    for j in range(1, NCH):
        gb_copy(j).start()
    gb_r[0, mine, :] = grad_bef[:, 0:128]
    gb_r[1, mine, :] = grad_bef[:, 128:256]
    for j in range(1, NCH):
        gb_copy(j).wait_recv()

    def grads(i, _):
        t = NSEC - 1 - i
        turned = pltpu.roll(gb_r[t // 8], lax.rem(128 - 16 * (t % 8), 128), 1)[:, 0:UNITS]
        grad_bef = turned.astype(BF16)
        g = g_ref[...]
        xhat = xhat_ref[t]
        to, at = (t // 2) % 2, 2 * (t // 4) + t % 2
        parts_ref[to, 0, at] = dot(grad_bef, xhat, TN).astype(BF16)
        parts_ref[to, 1, at] = dot(act_ref[t], g.astype(BF16), TN).astype(BF16)
        c2 = jnp.sum(turned * bef_ref[t], axis=1, keepdims=True) * (1.0 / WIDTH)
        g_ref[...] = g + rstd_ref[t] * (dot(grad_bef, wdc_all[t]) - xhat.astype(F32) * c2)
        return 0

    lax.fori_loop(0, NSEC, grads, 0)

    for x_to in range(2):
        part_copy(x_to, hid_s, hid_r, sem_hs, sem_hr, False)
        part_copy(x_to, cot_s, cot_r, sem_cs, sem_cr, False)

    def data_left(j, _):
        for copy in data_copies(j):
            copy.wait_send()
        return 0

    lax.fori_loop(1, NSEC, data_left, 0)

    def group_left(s, _):
        for j in range(1, NCH):
            stat_copy(s, j).wait_send()
            mix_copy(s, j).wait_send()
        return 0

    lax.fori_loop(0, NSEC, group_left, 0)
    for j in range(1, NCH):
        cw_copy(j).wait_send()
        gb_copy(j).wait_send()


def sections_call(ids, hid, cot, store, exps, gains, wd, wu):
    vmem = pl.BlockSpec(memory_space=pltpu.VMEM)
    dma = pltpu.SemaphoreType.DMA
    return pl.pallas_call(
        sections_kernel,
        name="sections",
        out_shape=jax.ShapeDtypeStruct((2, 2, NCH, UNITS, CH), BF16),
        in_specs=[pl.BlockSpec(memory_space=pltpu.SMEM), vmem, vmem,
                  pl.BlockSpec(memory_space=pl.ANY), vmem, vmem, vmem, vmem],
        out_specs=vmem,
        scratch_shapes=[
            pltpu.VMEM((8, 16, 640), BF16), pltpu.VMEM((8, 16, 640), BF16),
            pltpu.VMEM((8, 16, 128), BF16), pltpu.VMEM((2 * UNITS, WIDTH), BF16),
            pltpu.VMEM((UNITS, 128), F32),
            pltpu.VMEM((2, 4, 16, 640), BF16), pltpu.VMEM((2, 4, 16, 640), BF16),
            pltpu.VMEM((NSEC, 4, 16, 128), BF16), pltpu.VMEM((NSEC, 2 * UNITS, CH), BF16),
            pltpu.VMEM((NSEC, UNITS, 128), F32), pltpu.VMEM((NSEC, 4, 16, CH), BF16),
            pltpu.VMEM((128, CH), BF16), pltpu.VMEM((256, CH), BF16), pltpu.VMEM((256, CH), BF16),
            pltpu.VMEM((NSEC, UNITS, CH), BF16), pltpu.VMEM((ROWS, CH), F32),
            pltpu.VMEM((ROWS, CH), F32), pltpu.VMEM((ROWS, CH), F32),
            pltpu.VMEM((ROWS, 128), F32), pltpu.VMEM((ROWS, 128), F32),
            pltpu.VMEM((2, ROWS, 128), F32), pltpu.VMEM((NSEC, ROWS, UNITS), F32),
            pltpu.VMEM((NSEC, ROWS, UNITS), BF16),
            pltpu.VMEM((NSEC, ROWS, 1), F32), pltpu.VMEM((NSEC, ROWS, 1), F32),
            pltpu.VMEM((NSEC, ROWS, CH), BF16),
            pltpu.VMEM((NSEC, 16, 128), F32), pltpu.VMEM((NSEC, NCH - 1, 16, 128), F32),
            pltpu.VMEM((NSEC, NCH, 24, 256), F32), pltpu.VMEM((NSEC, NCH - 1, 24, 256), F32),
            pltpu.VMEM((ROWS, 256), F32), pltpu.VMEM((NCH - 1, 8, 256), F32),
            pltpu.VMEM((256, 256), BF16), pltpu.VMEM((NSEC, 8, 256), F32),
            pltpu.VMEM((2, 8, 128), F32), pltpu.VMEM((2, ROWS, 128), F32),
            dma((2,)), dma((2,)), dma((2,)), dma((2,)), dma((4, NSEC)),
            dma((NSEC,)), dma((NSEC,)), dma((NSEC,)), dma((NSEC,)),
            dma((NSEC, NCH - 1)), dma((NSEC, NCH - 1)), dma((NSEC, NCH - 1)), dma((NSEC, NCH - 1)),
            dma((NCH - 1,)), dma((NCH - 1,)), dma((NCH - 1,)), dma((NCH - 1,)),
        ],
        compiler_params=pltpu.CompilerParams(
            collective_id=1, has_side_effects=True, vmem_limit_bytes=56 * 2**20
        ),
    )(ids, hid, cot, store, exps, gains, wd, wu)


def reduce_kernel(
    parts_ref, gains_ref, down_ref, up_ref,
    x_r, z_s, z_r, f_s, a_r, b_r,
    sem_xs, sem_xr, sem_zs, sem_zr, sem_as, sem_ar, sem_bs, sem_br,
):
    me = lax.axis_index("segment")
    dp = lax.axis_index("dp")
    y, xh, core = me // 4, (me // 2) % 2, me % 2
    z, xl = dp // 2, dp % 2
    chunk = 2 * y + core

    def seg_of(q):
        return 4 * (q // 2) + 2 * xh + q % 2

    goal = seg_of(z // 2)
    near = [(a, b) for a in range(2) for b in range(2) if (a, b) != (0, 0)]

    def x_device(a, b):
        return (4 * y + 2 * lax.rem(xh + a, 2) + core, 2 * z + lax.rem(xl + b, 2))

    barrier = pltpu.get_barrier_semaphore()

    def greet(device):
        pl.semaphore_signal(barrier, inc=1, device_id=device, device_id_type=MESH)

    for a, b in near:
        greet(x_device(a, b))

    def greet_z(j, _):
        greet((me, 2 * lax.rem(z + j, NZ) + xl))
        return 0

    lax.fori_loop(1, NZ, greet_z, 0)

    def greet_goal(j, _):
        @pl.when((goal != me) | (j != z))
        def _():
            greet((goal, 2 * j + xl))

        source, at = seg_of(j // 2), 2 * chunk + j % 2

        @pl.when((source != me) | (at != z))
        def _():
            greet((source, 2 * at + xl))

        return 0

    lax.fori_loop(0, NZ, greet_goal, 0)
    pl.semaphore_wait(
        barrier, len(near) + NZ - 1 + 2 * NZ - 2 * jnp.where(goal == me, 1, 0)
    )

    def x_copy(k, i):
        a, b = near[k]
        to_xh, to_xl = lax.rem(xh + a, 2), lax.rem(xl + b, 2)
        return pltpu.make_async_remote_copy(
            src_ref=parts_ref.at[to_xh, to_xl, i], dst_ref=x_r.at[k, i],
            send_sem=sem_xs.at[k, i], recv_sem=sem_xr.at[k, i],
            device_id=x_device(a, b), device_id_type=MESH,
        )

    def x_send(n, _):
        for k in range(3):
            x_copy(k, NCH - 1 - n).start()
        return 0

    lax.fori_loop(0, NCH, x_send, 0)

    def z_copy(i, h):
        to = 2 * i + h
        step = lax.rem(to - z + NZ, NZ)
        return to, pltpu.make_async_remote_copy(
            src_ref=z_s.at[i, :, 512 * h : 512 * h + 640], dst_ref=z_r.at[step],
            send_sem=sem_zs.at[to], recv_sem=sem_zr.at[step],
            device_id=(me, 2 * to + xl), device_id_type=MESH,
        )

    def z_send(n, _):
        i = NCH - 1 - n
        total = parts_ref[xh, xl, i].astype(F32)
        for k in range(3):
            x_copy(k, i).wait_recv()
            total = total + x_r[k, i].astype(F32)
        z_s[i] = total.astype(BF16)
        for h in range(2):
            to, copy = z_copy(i, h)

            @pl.when(to != z)
            def _():
                copy.start()

        return 0

    lax.fori_loop(0, NCH, z_send, 0)
    f_total = z_s[z // 2, :, pl.ds(pl.multiple_of(512 * (z % 2), 128), 640)].astype(F32)

    def z_recv(step, total):
        pltpu.make_async_copy(z_r.at[step], z_r.at[step], sem_zr.at[step]).wait()
        return total + z_r[step].astype(F32)

    f_s[...] = lax.fori_loop(1, NZ, z_recv, f_total).astype(BF16)

    half = z % 2

    def a_copy(to):
        return pltpu.make_async_remote_copy(
            src_ref=f_s, dst_ref=a_r.at[chunk, half], send_sem=sem_as.at[to],
            recv_sem=sem_ar.at[chunk, half], device_id=(goal, 2 * to + xl), device_id_type=MESH,
        )

    def a_send(j, _):
        to = lax.rem(z + j, NZ)

        @pl.when((goal != me) | (to != z))
        def _():
            a_copy(to).start()

        @pl.when((goal == me) & (to == z))
        def _():
            pltpu.make_async_copy(f_s, a_r.at[chunk, half], sem_ar.at[chunk, half]).start()

        return 0

    lax.fori_loop(0, NZ, a_send, 0)

    def b_copy(q, h):
        return pltpu.make_async_remote_copy(
            src_ref=a_r.at[q, h], dst_ref=b_r.at[q, h], send_sem=sem_bs.at[q, h],
            recv_sem=sem_br.at[q, h], device_id=(me, 2 * z + 1 - xl), device_id_type=MESH,
        )

    for q in range(NCH):
        for h in range(2):
            pltpu.make_async_copy(a_r.at[q, h], a_r.at[q, h], sem_ar.at[q, h]).wait()
            b_copy(q, h).start()

    for q in range(NCH):
        for h in range(2):
            b_copy(q, h).wait_recv()
            low, cols = (0, slice(CH * q, CH * q + 640)) if h == 0 else (
                128, slice(CH * q + 640, CH * q + CH))
            own, other = a_r[q, h][:, low:], b_r[q, h][:, low:]
            down = jnp.where(xl == 0, own, other)
            up_ref[:, cols] = jnp.where(xl == 0, other, own)
            down_ref[:, cols] = (down.astype(F32) * gains_ref[:, cols].astype(F32)).astype(BF16)

    def x_left(i, _):
        for k in range(3):
            x_copy(k, i).wait_send()
        for h in range(2):
            to, copy = z_copy(i, h)

            @pl.when(to != z)
            def _():
                copy.wait_send()

        return 0

    lax.fori_loop(0, NCH, x_left, 0)

    def a_left(to, _):
        @pl.when((goal != me) | (to != z))
        def _():
            a_copy(to).wait_send()

        return 0

    lax.fori_loop(0, NZ, a_left, 0)
    for q in range(NCH):
        for h in range(2):
            b_copy(q, h).wait_send()


def reduce_call(parts, gains):
    vmem = pl.BlockSpec(memory_space=pltpu.VMEM)
    dma = pltpu.SemaphoreType.DMA
    out = jax.ShapeDtypeStruct((UNITS, WIDTH), BF16)
    return pl.pallas_call(
        reduce_kernel,
        name="reduce",
        out_shape=(out, out),
        in_specs=[vmem, vmem],
        out_specs=(vmem, vmem),
        scratch_shapes=[
            pltpu.VMEM((3, NCH, UNITS, CH), BF16), pltpu.VMEM((NCH, UNITS, CH), BF16),
            pltpu.VMEM((NZ, UNITS, 640), BF16), pltpu.VMEM((UNITS, 640), BF16),
            pltpu.VMEM((NCH, 2, UNITS, 640), BF16), pltpu.VMEM((NCH, 2, UNITS, 640), BF16),
            dma((3, NCH)), dma((3, NCH)), dma((NZ,)), dma((NZ,)), dma((NZ,)), dma((NCH, 2)),
            dma((NCH, 2)), dma((NCH, 2)),
        ],
        compiler_params=pltpu.CompilerParams(
            collective_id=2, has_side_effects=True, vmem_limit_bytes=56 * 2**20
        ),
    )(parts, gains)


def shards(hidden_in, cotangent, stored_bases, sample_ids, block_exps, ln_gains, w_down, w_up):
    parts = sections_call(
        sample_ids, hidden_in, cotangent, stored_bases[0], block_exps[0], ln_gains,
        jnp.swapaxes(w_down[0], 0, 1), w_up[0],
    )
    down, up = reduce_call(parts, ln_gains)
    return jnp.swapaxes(down, 0, 1)[None], up[None]


def solution(mesh):
    return jax.shard_map(
        shards,
        mesh=mesh,
        in_specs=(
            P(None, "dp", "segment"),
            P(None, "dp", "segment"),
            P("segment", None, "dp", None),
            P("dp", None),
            P("segment", None, "dp", None),
            P("segment", None),
            P("segment", None, None),
            P("segment", None, None),
        ),
        out_specs=(P("segment", None, None), P("segment", None, None)),
        check_vma=False,
    )
```

```python
import functools

import jax
import jax.numpy as jnp
from jax import lax
from jax.experimental import pallas as pl
from jax.experimental.pallas import tpu as pltpu
from jax.sharding import PartitionSpec as P

MESH = pl.DeviceIdType.MESH
F32 = jnp.float32
BF16 = jnp.bfloat16
NSEC = 16
UNITS = 16
NCH = 8
CH = 1152
WIDTH = NCH * CH
PART = 576
NZ = 16
ROWS = 64
HALF = 32
NT = (((1,), (1,)), ((), ()))
TN = (((0,), (0,)), ((), ()))
K_GELU = 0.7978845608028654
C_GELU = 0.044715


def dot(a, b, dims=(((1,), (0,)), ((), ()))):
    return lax.dot_general(a, b, dims, preferred_element_type=F32)


def lanes(shape):
    return lax.broadcasted_iota(jnp.int32, shape, len(shape) - 1)


def gelu(x):
    return 0.5 * x * (1.0 + jnp.tanh(K_GELU * (x + C_GELU * x * x * x)))


def gelu_slope(x):
    th = jnp.tanh(K_GELU * (x + C_GELU * x * x * x))
    return 0.5 * (1.0 + th) + 0.5 * x * (1.0 - th * th) * K_GELU * (1.0 + 3.0 * C_GELU * x * x)


def power_of_two(exps):
    factor = jnp.ones(exps.shape, F32)
    for bit in range(5):
        factor = jnp.where(((-exps) >> bit) & 1 == 1, factor * F32(0.5 ** (1 << bit)), factor)
    return factor


def join_parts(ref):
    first = ref[0].reshape(ROWS, 640).astype(F32)
    second = ref[1].reshape(ROWS, 640).astype(F32)
    lane = lanes((ROWS, 128))
    turned = [pltpu.roll(second[:, 128 * i : 128 * i + 128], 64, 1) for i in range(5)]
    tiles = [first[:, 128 * i : 128 * i + 128] for i in range(4)]
    tiles.append(jnp.where(lane < 64, first[:, 512:640], turned[0]))
    for i in range(4):
        tiles.append(jnp.where(lane < 64, turned[i], turned[i + 1]))
    return jnp.concatenate(tiles, axis=1)


def held(ref, sem):
    pltpu.make_async_copy(ref, ref, sem).wait()


def kernel(
    ids_ref, hid_ref, cot_ref, store_ref, exps_ref, gains_ref, wd_ref, wu_ref,
    down_ref, up_ref,
    hid_s, cot_s, wts_s, fx_s, hid_r, cot_r, wts_r, fx_r, base_r,
    spread, factor_ref, scale_ref, wu_all, wuc_all, wdc_all, a_ref, g_ref, d_ref, cen_ref,
    pay, bpad, bef_all, bef_ref, act_ref, mean_ref, rstd_ref, xhat_ref,
    stat_s, stat_r, mix_s, mix_r, cw_s, cw_r, gm_ref, xt_ref, gb_s, gb_r,
    parts, x_r, z_s, z_r, f_s, a_r, b_r,
    sem_hs, sem_hr, sem_cs, sem_cr, sem_ds, sem_fx, sem_wts, sem_base, sem_fw,
    sem_st_s, sem_st_r, sem_mx_s, sem_mx_r, sem_cw_s, sem_cw_r, sem_gb_s, sem_gb_r,
    sem_xs, sem_xr, sem_zs, sem_zr, sem_as, sem_ar, sem_bs, sem_br,
):
    me = lax.axis_index("segment")
    dp = lax.axis_index("dp")
    y, xh, core = me // 4, (me // 2) % 2, me % 2
    z, xl = dp // 2, dp % 2
    chunk = 2 * y + core

    def seg_of(q):
        return 4 * (q // 2) + 2 * xh + q % 2

    goal = seg_of(z // 2)
    mate = 2 * (z + 1 - 2 * (z % 2)) + xl

    barrier = pltpu.get_barrier_semaphore()

    def greet(device):
        pl.semaphore_signal(barrier, inc=1, device_id=device, device_id_type=MESH)

    def greet_lines(j, _):
        greet((lax.rem(me + j, NSEC), dp))
        greet((me, 2 * lax.rem(z + j, NZ) + xl))
        return 0

    lax.fori_loop(1, NSEC, greet_lines, 0)

    def x_device(a, b):
        return (4 * y + 2 * lax.rem(xh + a, 2) + core, 2 * z + lax.rem(xl + b, 2))

    for a, b in ((0, 1), (1, 0), (1, 1)):
        greet(x_device(a, b))

    def greet_goal(j, _):
        @pl.when((goal != me) | (j != z))
        def _():
            greet((goal, 2 * j + xl))

        source, at = seg_of(j // 2), 2 * chunk + j % 2

        @pl.when((source != me) | (at != z))
        def _():
            greet((source, 2 * at + xl))

        return 0

    lax.fori_loop(0, NZ, greet_goal, 0)

    hid_s[...] = jnp.zeros(hid_s.shape, BF16)
    cot_s[...] = jnp.zeros(cot_s.shape, BF16)
    lane16 = lanes((UNITS, 128))
    batches = []
    for slot in range(8):
        batch = jnp.int32(0)
        for k in range(8):
            batch = jnp.maximum(batch, jnp.where(ids_ref[0, k] == slot, k, 0))
        batches.append(batch)
        hid_s[slot, :, 0:PART] = hid_ref[batch]
        cot_s[slot, :, 0:PART] = cot_ref[batch]
    aux = jnp.zeros((UNITS, 128), F32)
    up_total = jnp.zeros((UNITS, 1), F32)
    down_total = jnp.zeros((UNITS, 1), F32)
    for q in range(NCH):
        part = slice(q * CH, (q + 1) * CH)
        scaled = (wd_ref[:, part].astype(F32) * gains_ref[:, part].astype(F32)).astype(BF16)
        wts_s[0:UNITS, part] = scaled
        up = wu_ref[:, part]
        wts_s[UNITS : 2 * UNITS, part] = up
        down_sum = jnp.sum(scaled.astype(F32), axis=1, keepdims=True)
        aux = aux + jnp.where(lane16 == 16 + q, down_sum, 0.0)
        down_total = down_total + down_sum
        up_total = up_total + jnp.sum(up.astype(F32), axis=1, keepdims=True)
    aux = aux + jnp.where(lane16 == 0, down_total * (1.0 / WIDTH), 0.0)
    aux = (aux + jnp.where(lane16 == 1, up_total * (1.0 / WIDTH), 0.0)).astype(BF16)
    bpad[...] = jnp.zeros(bpad.shape, F32)
    for x_to in range(2):
        picks = []
        for g in range(4):
            bpad[0:16, 0:72] = power_of_two(exps_ref[batches[4 * x_to + g]])
            picks.append(bpad[0:16, :])
        for q in range(NCH):
            packed = jnp.zeros((16, 128), F32)
            for g in range(4):
                turned = pltpu.roll(picks[g], (32 * g - 9 * q) % 128, 1)
                packed = jnp.where((lane16 >= 32 * g) & (lane16 < 32 * g + 9), turned, packed)
            fx_s[x_to, q, 0:16] = packed.astype(BF16)
            fx_s[x_to, q, 16:32] = aux

    pl.semaphore_wait(
        barrier, 2 * (NSEC - 1) + 3 + 2 * NZ - 2 * jnp.where(goal == me, 1, 0)
    )

    def part_copy(x_to, src, dst, send, recv, go):
        target = 4 * y + 2 * x_to + xh
        rows = src.at[4 * x_to : 4 * x_to + 4]

        if go:

            @pl.when(target == me)
            def _():
                pltpu.make_async_copy(rows, dst.at[core], recv.at[core]).start()

        @pl.when(target != me)
        def _():
            copy = pltpu.make_async_remote_copy(
                src_ref=rows, dst_ref=dst.at[core], send_sem=send.at[x_to],
                recv_sem=recv.at[core], device_id=(target, dp), device_id_type=MESH,
            )
            copy.start() if go else copy.wait_send()

    for x_to in range(2):
        part_copy(x_to, hid_s, hid_r, sem_hs, sem_hr, True)

    def place(target):
        to_chunk = 2 * (target // 4) + target % 2
        return (target // 2) % 2, to_chunk, pl.ds(pl.multiple_of(to_chunk * CH, 128), CH)

    def data_send(kind):
        def pair(target):
            x_to, to_chunk, cols = place(target)
            if kind == 0:
                return wts_s.at[:, cols], wts_r.at[me], sem_wts.at[me]
            if kind == 1:
                return fx_s.at[x_to, to_chunk], fx_r.at[me], sem_fx.at[me]
            return store_ref.at[pl.ds(4 * x_to, 4), :, cols], base_r.at[me], sem_base.at[me]

        def one(j, _):
            target = lax.rem(me + j, NSEC)
            src, dst, sem = pair(target)
            pltpu.make_async_remote_copy(
                src_ref=src, dst_ref=dst, send_sem=sem_ds.at[kind], recv_sem=sem,
                device_id=(target, dp), device_id_type=MESH,
            ).start()
            return 0

        src, dst, sem = pair(me)
        pltpu.make_async_copy(src, dst, sem).start()
        lax.fori_loop(1, NSEC, one, 0)

    direct = core == z % 2

    @pl.when(direct)
    def _():
        data_send(0)

    data_send(1)
    data_send(2)
    for x_to in range(2):
        part_copy(x_to, cot_s, cot_r, sem_cs, sem_cr, True)

    block = lax.broadcasted_iota(jnp.int32, (128, CH), 0)
    feature = lax.broadcasted_iota(jnp.int32, (128, CH), 1)
    spread[...] = jnp.where(block % 32 == feature // 128, 1.0, 0.0).astype(BF16)
    pay[...] = jnp.zeros(pay.shape, F32)
    bpad[...] = jnp.zeros(bpad.shape, F32)
    bef_all[...] = jnp.zeros(bef_all.shape, F32)
    wuc_all[...] = jnp.zeros(wuc_all.shape, BF16)

    def wts_on(n):
        s = 2 * n + z % 2
        return s, pltpu.make_async_remote_copy(
            src_ref=wts_r.at[s], dst_ref=wts_r.at[s], send_sem=sem_fw.at[n],
            recv_sem=sem_wts.at[s], device_id=(me, mate), device_id_type=MESH,
        )

    def pass_on(n, _):
        s, copy = wts_on(n)
        held(wts_r.at[s], sem_wts.at[s])
        copy.start()
        return 0

    lax.fori_loop(0, NSEC // 2, pass_on, 0)

    for h in range(2):
        held(hid_r.at[h], sem_hr.at[h])
    first = join_parts(hid_r)
    a_ref[0] = first[0:HALF]
    a_ref[1] = first[HALF:ROWS]

    lane = lanes((HALF, 128))
    lane64 = lanes((16, 128))

    def prefetch(s):
        held(fx_r.at[s], sem_fx.at[s])
        packed = fx_r[s, 0:16].astype(F32)
        small = jnp.concatenate(
            [jnp.where((lane64 >= 32 * g) & (lane64 < 32 * g + 9), packed, 0.0) for g in range(4)],
            axis=0,
        )
        inverse = jnp.where(small > 0.0, 1.0 / jnp.where(small > 0.0, small, 1.0), 0.0)
        factor_ref[...] = dot(small.astype(BF16), spread[...])
        scale_ref[...] = dot(inverse.astype(BF16), spread[...])

    def stat_copy(s, h, j):
        target = seg_of(lax.rem(chunk + j, NCH))
        return pltpu.make_async_remote_copy(
            src_ref=stat_s.at[s, h], dst_ref=stat_r.at[s, h, j - 1], send_sem=sem_st_s.at[s, h],
            recv_sem=sem_st_r.at[s, h], device_id=(target, dp), device_id_type=MESH,
        )

    def start(s, h):
        if h == 0:
            held(base_r.at[s], sem_base.at[s])

            @pl.when(s % 2 != z % 2)
            def _():
                held(wts_r.at[s], sem_wts.at[s])

        rows = slice(HALF * h, HALF * h + HALF)
        total = jnp.zeros((HALF, 128), F32)
        for i in range(CH // 128):
            cols = slice(128 * i, 128 * i + 128)
            base = base_r[s, 2 * h : 2 * h + 2, :, cols].reshape(HALF, 128).astype(F32)
            coded = ((a_ref[h, :, cols] - base) * scale_ref[rows, cols]).astype(BF16)
            decoded = base + jnp.clip(coded.astype(F32), -448.0, 448.0) * factor_ref[rows, cols]
            d_ref[s % 2, h, :, cols] = decoded
            total = total + decoded
        own_mean = jnp.sum(total, axis=1, keepdims=True) * (1.0 / CH)
        squares = jnp.zeros((HALF, 128), F32)
        for i in range(CH // 128):
            cols = slice(128 * i, 128 * i + 128)
            center = d_ref[s % 2, h, :, cols] - own_mean
            squares = squares + center * center
            cen_ref[h, :, cols] = center.astype(BF16)
        own_m2 = jnp.sum(squares, axis=1, keepdims=True)
        pay[h, :, 0:UNITS] = dot(cen_ref[h], wts_r[s, 0:UNITS, :], NT)
        row = jnp.where(lane == 16 + chunk, own_mean, pay[h])
        row = jnp.where(lane == 24, own_m2, row)
        packed = row[0:8]
        for g in range(1, 4):
            packed = packed + pltpu.roll(row[8 * g : 8 * g + 8], 32 * g, 1)
        stat_s[s, h] = packed
        for j in range(1, NCH):
            stat_copy(s, h, j).start()

    def finish(s, h):
        up = wts_r[s, UNITS : 2 * UNITS, :]
        held(stat_r.at[s, h], sem_st_r.at[s, h])
        total = stat_s[s, h]
        for j in range(NCH - 1):
            total = total + stat_r[s, h, j]
        rows = jnp.concatenate(
            [total] + [pltpu.roll(total, 128 - 32 * g, 1) for g in range(1, 4)], axis=0
        )
        is_mean = (lane >= 16) & (lane < 24)
        mean = jnp.sum(jnp.where(is_mean, rows, 0.0), axis=1, keepdims=True) * (1.0 / NCH)
        off = jnp.where(is_mean, rows - mean, 0.0)
        squares = jnp.sum(
            jnp.where(lane == 24, rows, 0.0) + CH * off * off, axis=1, keepdims=True
        )
        rstd = lax.rsqrt(squares * (1.0 / WIDTH) + 1e-05)
        shift = dot(off.astype(BF16), fx_r[s, 16:32], NT)
        before = (rows[:, 0:UNITS] + shift) * rstd
        act = gelu(before).astype(BF16)
        added = dot(act, up)
        a_ref[h] = (d_ref[s % 2, h] + added).astype(BF16).astype(F32)
        here = slice(HALF * h, HALF * h + HALF)
        bef_ref[s, here] = before
        act_ref[s, here] = act
        mean_ref[s, here] = mean
        rstd_ref[s, here] = rstd

    def mix_copy(s, j):
        to_chunk = lax.rem(chunk + j, NCH)
        return pltpu.make_async_remote_copy(
            src_ref=mix_s.at[s, to_chunk], dst_ref=mix_r.at[s, j - 1],
            send_sem=sem_mx_s.at[s], recv_sem=sem_mx_r.at[s],
            device_id=(seg_of(to_chunk), dp), device_id_type=MESH,
        )

    def side_work(s):
        decoded = d_ref[s % 2].reshape(ROWS, CH)
        xhat = ((decoded - mean_ref[s]) * rstd_ref[s]).astype(BF16)
        xhat_ref[s] = xhat
        ups = wuc_all[...]
        rows = dot(xhat, ups, NT)
        downs = (wts_r[s, 0:UNITS, :].astype(F32) - fx_r[s, 16:32, 0:1].astype(F32)).astype(BF16)
        wdc_all[s] = downs
        gram = dot(downs, ups, NT)
        for q in range(NCH):
            mix_s[s, q, 0:8] = rows[8 * q : 8 * q + 8]
            mix_s[s, q, 8:24] = gram
        for j in range(1, NCH):
            mix_copy(s, j).start()
        up = wts_r[s, UNITS : 2 * UNITS, :]
        own = pl.ds(pl.multiple_of(s * UNITS, UNITS), UNITS)
        wu_all[own, :] = up
        wuc_all[own, :] = (up.astype(F32) - fx_r[s, 16:32, 1:2].astype(F32)).astype(BF16)
        bpad[:, 0:UNITS] = bef_ref[s]
        bef_all[s // 8] = bef_all[s // 8] + pltpu.roll(bpad[...], 16 * (s % 8), 1)

    prefetch(0)
    for h in range(2):
        start(0, h)
    prefetch(1)

    def step(s, _):
        for h in range(2):
            finish(s, h)
            start(s + 1, h)
        side_work(s)

        @pl.when(s + 2 < NSEC)
        def _():
            prefetch(s + 2)

        return 0

    lax.fori_loop(0, NSEC - 1, step, 0)

    wu_all[(NSEC - 1) * UNITS : NSEC * UNITS, :] = wts_r[NSEC - 1, UNITS : 2 * UNITS, :]
    for h in range(2):
        held(cot_r.at[h], sem_cr.at[h])
    cot = join_parts(cot_r)
    g_ref[...] = cot
    cw_s[...] = dot(cot.astype(BF16), wu_all[...], NT)

    def cw_copy(j):
        to_chunk = lax.rem(chunk + j, NCH)
        return pltpu.make_async_remote_copy(
            src_ref=cw_s.at[pl.ds(pl.multiple_of(8 * to_chunk, 8), 8)], dst_ref=cw_r.at[j - 1],
            send_sem=sem_cw_s.at[0], recv_sem=sem_cw_r.at[0],
            device_id=(seg_of(to_chunk), dp), device_id_type=MESH,
        )

    for j in range(1, NCH):
        cw_copy(j).start()
    for h in range(2):
        finish(NSEC - 1, h)
    side_work(NSEC - 1)

    mine = pl.ds(pl.multiple_of(8 * chunk, 8), 8)

    def fold(t, _):
        held(mix_r.at[t], sem_mx_r.at[t])
        both = mix_s[t, chunk]
        for j in range(NCH - 1):
            both = both + mix_r[t, j]
        both = jnp.where(lanes((24, 256)) < UNITS * t, both, 0.0)
        xt_ref[t] = both[0:8]
        gm_ref[pl.ds(pl.multiple_of(t * UNITS, UNITS), UNITS), :] = both[8:24].astype(BF16)
        return 0

    held(cw_r, sem_cw_r.at[0])
    grad_act = cw_s[mine, :]
    for j in range(NCH - 1):
        grad_act = grad_act + cw_r[j]
    bef8 = jnp.concatenate([bef_all[0, mine, :], bef_all[1, mine, :]], axis=1)
    slope8 = gelu_slope(bef8)
    lane8 = lanes((8, 256))
    lax.fori_loop(0, NSEC, fold, 0)

    def back(i, carry):
        grad_act, out = carry
        t = NSEC - 1 - i
        here = (lane8 >= UNITS * t) & (lane8 < UNITS * t + UNITS)
        grad_bef = jnp.where(here, grad_act * slope8, 0.0).astype(BF16)
        wide = grad_bef.astype(F32)
        c2 = jnp.sum(wide * bef8, axis=1, keepdims=True) * (1.0 / WIDTH)
        change = dot(grad_bef, gm_ref[...]) - c2 * xt_ref[t]
        return grad_act + rstd_ref[t, mine, :] * change, out + wide

    _, grad_bef = lax.fori_loop(0, NSEC, back, (grad_act, jnp.zeros((8, 256), F32)))
    gb_s[0] = grad_bef[:, 0:128]
    gb_s[1] = grad_bef[:, 128:256]

    def gb_copy(j):
        target = seg_of(lax.rem(chunk + j, NCH))
        return pltpu.make_async_remote_copy(
            src_ref=gb_s, dst_ref=gb_r.at[:, mine], send_sem=sem_gb_s.at[0],
            recv_sem=sem_gb_r.at[0], device_id=(target, dp), device_id_type=MESH,
        )

    for j in range(1, NCH):
        gb_copy(j).start()
    gb_r[0, mine, :] = grad_bef[:, 0:128]
    gb_r[1, mine, :] = grad_bef[:, 128:256]
    held(gb_r.at[:, 0 : ROWS - 8], sem_gb_r.at[0])

    def x_copy(t, kind):
        to, at = (t // 2) % 2, 2 * (t // 4) + t % 2
        a, b = lax.rem(to + xh, 2), lax.rem(kind + xl, 2)
        slot = jnp.maximum(2 * a + b - 1, 0)
        return 2 * a + b, pltpu.make_async_remote_copy(
            src_ref=parts.at[to, kind, at], dst_ref=x_r.at[at, slot], send_sem=sem_xs.at[t, kind],
            recv_sem=sem_xr.at[at], device_id=(4 * y + 2 * to + core, 2 * z + kind),
            device_id_type=MESH,
        )

    def grads(i, _):
        t = NSEC - 1 - i
        to, at = (t // 2) % 2, 2 * (t // 4) + t % 2
        turned = pltpu.roll(gb_r[t // 8], lax.rem(128 - 16 * (t % 8), 128), 1)[:, 0:UNITS]
        grad_bef = turned.astype(BF16)
        g = g_ref[...]
        xhat = xhat_ref[t]
        parts[to, 0, at] = dot(grad_bef, xhat, TN).astype(BF16)
        parts[to, 1, at] = dot(act_ref[t], g.astype(BF16), TN).astype(BF16)
        for kind in range(2):
            away, copy = x_copy(t, kind)

            @pl.when(away > 0)
            def _():
                copy.start()

        c2 = jnp.sum(turned * bef_ref[t], axis=1, keepdims=True) * (1.0 / WIDTH)
        g_ref[...] = g + rstd_ref[t] * (dot(grad_bef, wdc_all[t]) - xhat.astype(F32) * c2)
        return 0

    lax.fori_loop(0, NSEC, grads, 0)

    def z_copy(i, h):
        to = 2 * i + h
        ahead = lax.rem(to - z + NZ, NZ)
        return to, pltpu.make_async_remote_copy(
            src_ref=z_s.at[i, :, 512 * h : 512 * h + 640], dst_ref=z_r.at[ahead],
            send_sem=sem_zs.at[to], recv_sem=sem_zr.at[0],
            device_id=(me, 2 * to + xl), device_id_type=MESH,
        )

    def z_send(n, _):
        i = NCH - 1 - n
        total = parts[xh, xl, i].astype(F32)
        held(x_r.at[i], sem_xr.at[i])
        for k in range(3):
            total = total + x_r[i, k].astype(F32)
        z_s[i] = total.astype(BF16)
        for h in range(2):
            to, copy = z_copy(i, h)

            @pl.when(to != z)
            def _():
                copy.start()

        return 0

    lax.fori_loop(0, NCH, z_send, 0)
    half = z % 2
    f_total = z_s[z // 2, :, pl.ds(pl.multiple_of(512 * half, 128), 640)].astype(F32)
    held(z_r.at[1:NZ], sem_zr.at[0])
    f_s[...] = lax.fori_loop(
        1, NZ, lambda n, total: total + z_r[n].astype(F32), f_total
    ).astype(BF16)

    def a_copy(to):
        return pltpu.make_async_remote_copy(
            src_ref=f_s, dst_ref=a_r.at[chunk, half], send_sem=sem_as.at[to],
            recv_sem=sem_ar.at[chunk, half], device_id=(goal, 2 * to + xl), device_id_type=MESH,
        )

    def a_send(j, _):
        to = lax.rem(z + j, NZ)

        @pl.when((goal != me) | (to != z))
        def _():
            a_copy(to).start()

        @pl.when((goal == me) & (to == z))
        def _():
            pltpu.make_async_copy(f_s, a_r.at[chunk, half], sem_ar.at[chunk, half]).start()

        return 0

    lax.fori_loop(0, NZ, a_send, 0)

    def b_copy(q, h):
        return pltpu.make_async_remote_copy(
            src_ref=a_r.at[q, h], dst_ref=b_r.at[q, h], send_sem=sem_bs.at[q, h],
            recv_sem=sem_br.at[q, h], device_id=(me, 2 * z + 1 - xl), device_id_type=MESH,
        )

    for q in range(NCH):
        for h in range(2):
            held(a_r.at[q, h], sem_ar.at[q, h])
            b_copy(q, h).start()

    for x_to in range(2):
        part_copy(x_to, hid_s, hid_r, sem_hs, sem_hr, False)
        part_copy(x_to, cot_s, cot_r, sem_cs, sem_cr, False)

    @pl.when(direct)
    def _():
        held(wts_r.at[0 : NSEC - 1], sem_ds.at[0])

    held(fx_r.at[0 : NSEC - 1], sem_ds.at[1])
    held(base_r.at[0 : NSEC - 1], sem_ds.at[2])

    def forwarded(n, _):
        wts_on(n)[1].wait_send()
        return 0

    lax.fori_loop(0, NSEC // 2, forwarded, 0)

    def left(s, _):
        for h in range(2):
            held(stat_r.at[s, h], sem_st_s.at[s, h])
        held(mix_r.at[s], sem_mx_s.at[s])
        for kind in range(2):
            away, copy = x_copy(s, kind)

            @pl.when(away > 0)
            def _():
                copy.wait_send()

        return 0

    lax.fori_loop(0, NSEC, left, 0)
    held(cw_r, sem_cw_s.at[0])
    held(gb_r.at[:, 0 : ROWS - 8], sem_gb_s.at[0])

    def z_left(i, _):
        for h in range(2):
            to, copy = z_copy(i, h)

            @pl.when(to != z)
            def _():
                copy.wait_send()

        return 0

    lax.fori_loop(0, NCH, z_left, 0)

    def a_left(to, _):
        @pl.when((goal != me) | (to != z))
        def _():
            a_copy(to).wait_send()

        return 0

    lax.fori_loop(0, NZ, a_left, 0)

    for q in range(NCH):
        for h in range(2):
            b_copy(q, h).wait_recv()
            low, cols = (0, slice(CH * q, CH * q + 640)) if h == 0 else (
                128, slice(CH * q + 640, CH * q + CH))
            own, other = a_r[q, h][:, low:], b_r[q, h][:, low:]
            down = jnp.where(xl == 0, own, other)
            up_ref[:, cols] = jnp.where(xl == 0, other, own)
            down_ref[:, cols] = (down.astype(F32) * gains_ref[:, cols].astype(F32)).astype(BF16)
    for q in range(NCH):
        for h in range(2):
            b_copy(q, h).wait_send()


def whole_call(ids, hid, cot, store, exps, gains, wd, wu):
    vmem = pl.BlockSpec(memory_space=pltpu.VMEM)
    dma = pltpu.SemaphoreType.DMA

    def bf(*shape):
        return pltpu.VMEM(shape, BF16)

    def f32(*shape):
        return pltpu.VMEM(shape, F32)

    out = jax.ShapeDtypeStruct((UNITS, WIDTH), BF16)
    peers = NCH - 1
    return pl.pallas_call(
        kernel,
        name="sections",
        out_shape=(out, out),
        in_specs=[pl.BlockSpec(memory_space=pltpu.SMEM), vmem, vmem,
                  pl.BlockSpec(memory_space=pl.ANY), vmem, vmem, vmem, vmem],
        out_specs=(vmem, vmem),
        scratch_shapes=[
            bf(8, 16, 640), bf(8, 16, 640), bf(2 * UNITS, WIDTH), bf(2, NCH, 32, 128),
            bf(2, 4, 16, 640), bf(2, 4, 16, 640), bf(NSEC, 2 * UNITS, CH), bf(NSEC, 32, 128),
            bf(NSEC, 4, 16, CH),
            bf(128, CH), f32(ROWS, CH), f32(ROWS, CH), bf(256, CH), bf(256, CH),
            bf(NSEC, UNITS, CH), f32(2, HALF, CH), f32(ROWS, CH), f32(2, 2, HALF, CH),
            bf(2, HALF, CH),
            f32(2, HALF, 128), f32(ROWS, 128), f32(2, ROWS, 128), f32(NSEC, ROWS, UNITS),
            bf(NSEC, ROWS, UNITS), f32(NSEC, ROWS, 1), f32(NSEC, ROWS, 1), bf(NSEC, ROWS, CH),
            f32(NSEC, 2, 8, 128), f32(NSEC, 2, peers, 8, 128),
            f32(NSEC, NCH, 24, 256), f32(NSEC, peers, 24, 256),
            f32(ROWS, 256), f32(peers, 8, 256), bf(256, 256), f32(NSEC, 8, 256),
            f32(2, 8, 128), f32(2, ROWS, 128),
            bf(2, 2, NCH, UNITS, CH), bf(NCH, 3, UNITS, CH), bf(NCH, UNITS, CH),
            bf(NZ, UNITS, 640), bf(UNITS, 640), bf(NCH, 2, UNITS, 640), bf(NCH, 2, UNITS, 640),
            dma((2,)), dma((2,)), dma((2,)), dma((2,)), dma((3,)), dma((NSEC,)), dma((NSEC,)),
            dma((NSEC,)), dma((NSEC // 2,)),
            dma((NSEC, 2)), dma((NSEC, 2)), dma((NSEC,)), dma((NSEC,)), dma((1,)), dma((1,)),
            dma((1,)), dma((1,)),
            dma((NSEC, 2)), dma((NCH,)), dma((NZ,)), dma((1,)), dma((NZ,)), dma((NCH, 2)),
            dma((NCH, 2)), dma((NCH, 2)),
        ],
        compiler_params=pltpu.CompilerParams(
            collective_id=1, has_side_effects=True, vmem_limit_bytes=56 * 2**20
        ),
    )(ids, hid, cot, store, exps, gains, wd, wu)


def shards(hidden_in, cotangent, stored_bases, sample_ids, block_exps, ln_gains, w_down, w_up):
    down, up = whole_call(
        sample_ids, hidden_in, cotangent, stored_bases[0], block_exps[0], ln_gains,
        jnp.swapaxes(w_down[0], 0, 1), w_up[0],
    )
    return jnp.swapaxes(down, 0, 1)[None], up[None]


def solution(mesh):
    return jax.shard_map(
        shards,
        mesh=mesh,
        in_specs=(
            P(None, "dp", "segment"),
            P(None, "dp", "segment"),
            P("segment", None, "dp", None),
            P("dp", None),
            P("segment", None, "dp", None),
            P("segment", None),
            P("segment", None, None),
            P("segment", None, None),
        ),
        out_specs=(P("segment", None, None), P("segment", None, None)),
        check_vma=False,
    )
```

```python
import functools

import jax
import jax.numpy as jnp
from jax import lax
from jax.experimental import pallas as pl
from jax.experimental.pallas import tpu as pltpu
from jax.sharding import PartitionSpec as P

MESH = pl.DeviceIdType.MESH
F32 = jnp.float32
BF16 = jnp.bfloat16
NSEC = 16
UNITS = 16
NCH = 8
CH = 1152
WIDTH = NCH * CH
PART = 576
NZ = 16
ROWS = 64
HALF = 32
NT = (((1,), (1,)), ((), ()))
TN = (((0,), (0,)), ((), ()))
K_GELU = 0.7978845608028654
C_GELU = 0.044715


def dot(a, b, dims=(((1,), (0,)), ((), ()))):
    return lax.dot_general(a, b, dims, preferred_element_type=F32)


def lanes(shape):
    return lax.broadcasted_iota(jnp.int32, shape, len(shape) - 1)


def gelu(x):
    return 0.5 * x * (1.0 + jnp.tanh(K_GELU * (x + C_GELU * x * x * x)))


def gelu_slope(x):
    th = jnp.tanh(K_GELU * (x + C_GELU * x * x * x))
    return 0.5 * (1.0 + th) + 0.5 * x * (1.0 - th * th) * K_GELU * (1.0 + 3.0 * C_GELU * x * x)


def power_of_two(exps):
    factor = jnp.ones(exps.shape, F32)
    for bit in range(5):
        factor = jnp.where(((-exps) >> bit) & 1 == 1, factor * F32(0.5 ** (1 << bit)), factor)
    return factor


def join_parts(ref):
    first = ref[0].reshape(ROWS, 640).astype(F32)
    second = ref[1].reshape(ROWS, 640).astype(F32)
    lane = lanes((ROWS, 128))
    turned = [pltpu.roll(second[:, 128 * i : 128 * i + 128], 64, 1) for i in range(5)]
    tiles = [first[:, 128 * i : 128 * i + 128] for i in range(4)]
    tiles.append(jnp.where(lane < 64, first[:, 512:640], turned[0]))
    for i in range(4):
        tiles.append(jnp.where(lane < 64, turned[i], turned[i + 1]))
    return jnp.concatenate(tiles, axis=1)


def held(ref, sem):
    pltpu.make_async_copy(ref, ref, sem).wait()


def kernel(
    ids_ref, hid_ref, cot_ref, store_ref, exps_ref, gains_ref, wd_ref, wu_ref,
    down_ref, up_ref,
    hid_s, cot_s, wts_s, fx_s, hid_r, cot_r, wts_r, fx_r, base_r,
    spread, factor_ref, scale_ref, wu_all, wuc_all, wdc_all, a_ref, g_ref, d_ref, cen_ref,
    pay, bpad, bef_all, bef_ref, act_ref, mean_ref, rstd_ref, xhat_ref,
    stat_s, stat_r, mix_s, mix_r, cw_s, cw_r, gram_s, gram_r, gm_ref, xt_ref, gb_s, gb_r,
    parts, x_r, z_s, z_r, f_s, a_r, b_r,
    sem_hs, sem_hr, sem_cs, sem_cr, sem_ds, sem_fx, sem_wts, sem_base, sem_fw,
    sem_st_s, sem_st_r, sem_mx_s, sem_mx_r, sem_cw_s, sem_cw_r, sem_gr_s, sem_gr_r,
    sem_gm_s, sem_gm_r, sem_gb_s, sem_gb_r,
    sem_xs, sem_xr, sem_zs, sem_zr, sem_as, sem_ar, sem_bs, sem_br,
):
    me = lax.axis_index("segment")
    dp = lax.axis_index("dp")
    y, xh, core = me // 4, (me // 2) % 2, me % 2
    z, xl = dp // 2, dp % 2
    chunk = 2 * y + core

    def seg_of(q):
        return 4 * (q // 2) + 2 * xh + q % 2

    peer_chunks = [lax.rem(chunk + j, NCH) for j in range(NCH)]
    peer_segs = [seg_of(q) for q in peer_chunks]
    goal = seg_of(z // 2)
    mate = 2 * (z + 1 - 2 * (z % 2)) + xl

    barrier = pltpu.get_barrier_semaphore()

    def greet(device):
        pl.semaphore_signal(barrier, inc=1, device_id=device, device_id_type=MESH)

    def greet_lines(j, _):
        greet((lax.rem(me + j, NSEC), dp))
        greet((me, 2 * lax.rem(z + j, NZ) + xl))
        return 0

    lax.fori_loop(1, NSEC, greet_lines, 0)

    def x_device(a, b):
        return (4 * y + 2 * lax.rem(xh + a, 2) + core, 2 * z + lax.rem(xl + b, 2))

    for a, b in ((0, 1), (1, 0), (1, 1)):
        greet(x_device(a, b))

    def greet_goal(j, _):
        @pl.when((goal != me) | (j != z))
        def _():
            greet((goal, 2 * j + xl))

        source, at = seg_of(j // 2), 2 * chunk + j % 2

        @pl.when((source != me) | (at != z))
        def _():
            greet((source, 2 * at + xl))

        return 0

    lax.fori_loop(0, NZ, greet_goal, 0)

    hid_s[...] = jnp.zeros(hid_s.shape, BF16)
    cot_s[...] = jnp.zeros(cot_s.shape, BF16)
    lane16 = lanes((UNITS, 128))
    batches = []
    for slot in range(8):
        batch = jnp.int32(0)
        for k in range(8):
            batch = jnp.maximum(batch, jnp.where(ids_ref[0, k] == slot, k, 0))
        batches.append(batch)
        hid_s[slot, :, 0:PART] = hid_ref[batch]
        cot_s[slot, :, 0:PART] = cot_ref[batch]
    aux = jnp.zeros((UNITS, 128), F32)
    up_total = jnp.zeros((UNITS, 1), F32)
    down_total = jnp.zeros((UNITS, 1), F32)
    for q in range(NCH):
        part = slice(q * CH, (q + 1) * CH)
        scaled = (wd_ref[:, part].astype(F32) * gains_ref[:, part].astype(F32)).astype(BF16)
        wts_s[0:UNITS, part] = scaled
        up = wu_ref[:, part]
        wts_s[UNITS : 2 * UNITS, part] = up
        down_sum = jnp.sum(scaled.astype(F32), axis=1, keepdims=True)
        aux = aux + jnp.where(lane16 == 16 + q, down_sum, 0.0)
        down_total = down_total + down_sum
        up_total = up_total + jnp.sum(up.astype(F32), axis=1, keepdims=True)
    aux = aux + jnp.where(lane16 == 0, down_total * (1.0 / WIDTH), 0.0)
    aux = (aux + jnp.where(lane16 == 1, up_total * (1.0 / WIDTH), 0.0)).astype(BF16)
    bpad[...] = jnp.zeros(bpad.shape, F32)
    for x_to in range(2):
        picks = []
        for g in range(4):
            bpad[0:16, 0:72] = power_of_two(exps_ref[batches[4 * x_to + g]])
            picks.append(bpad[0:16, :])
        for q in range(NCH):
            packed = jnp.zeros((16, 128), F32)
            for g in range(4):
                turned = pltpu.roll(picks[g], (32 * g - 9 * q) % 128, 1)
                packed = jnp.where((lane16 >= 32 * g) & (lane16 < 32 * g + 9), turned, packed)
            fx_s[x_to, q, 0:16] = packed.astype(BF16)
            fx_s[x_to, q, 16:32] = aux

    pl.semaphore_wait(
        barrier, 2 * (NSEC - 1) + 3 + 2 * NZ - 2 * jnp.where(goal == me, 1, 0)
    )

    def part_copy(x_to, src, dst, send, recv, go):
        target = 4 * y + 2 * x_to + xh
        rows = src.at[4 * x_to : 4 * x_to + 4]

        if go:

            @pl.when(target == me)
            def _():
                pltpu.make_async_copy(rows, dst.at[core], recv.at[core]).start()

        @pl.when(target != me)
        def _():
            copy = pltpu.make_async_remote_copy(
                src_ref=rows, dst_ref=dst.at[core], send_sem=send.at[x_to],
                recv_sem=recv.at[core], device_id=(target, dp), device_id_type=MESH,
            )
            copy.start() if go else copy.wait_send()

    for x_to in range(2):
        part_copy(x_to, hid_s, hid_r, sem_hs, sem_hr, True)

    def place(target):
        to_chunk = 2 * (target // 4) + target % 2
        return (target // 2) % 2, to_chunk, pl.ds(pl.multiple_of(to_chunk * CH, 128), CH)

    def data_send(kind):
        def pair(target):
            x_to, to_chunk, cols = place(target)
            if kind == 0:
                return wts_s.at[:, cols], wts_r.at[me], sem_wts.at[me]
            if kind == 1:
                return fx_s.at[x_to, to_chunk], fx_r.at[me], sem_fx.at[me]
            return store_ref.at[pl.ds(4 * x_to, 4), :, cols], base_r.at[me], sem_base.at[me]

        def one(j, _):
            target = lax.rem(me + j, NSEC)
            src, dst, sem = pair(target)
            pltpu.make_async_remote_copy(
                src_ref=src, dst_ref=dst, send_sem=sem_ds.at[kind], recv_sem=sem,
                device_id=(target, dp), device_id_type=MESH,
            ).start()
            return 0

        src, dst, sem = pair(me)
        pltpu.make_async_copy(src, dst, sem).start()
        lax.fori_loop(1, NSEC, one, 0)

    direct = core == z % 2

    @pl.when(direct)
    def _():
        data_send(0)

    data_send(1)
    data_send(2)
    for x_to in range(2):
        part_copy(x_to, cot_s, cot_r, sem_cs, sem_cr, True)

    block = lax.broadcasted_iota(jnp.int32, (128, CH), 0)
    feature = lax.broadcasted_iota(jnp.int32, (128, CH), 1)
    spread[...] = jnp.where(block % 32 == feature // 128, 1.0, 0.0).astype(BF16)
    pay[...] = jnp.zeros(pay.shape, F32)
    bpad[...] = jnp.zeros(bpad.shape, F32)
    bef_all[...] = jnp.zeros(bef_all.shape, F32)

    def wts_on(n):
        s = 2 * n + z % 2
        return s, pltpu.make_async_remote_copy(
            src_ref=wts_r.at[s], dst_ref=wts_r.at[s], send_sem=sem_fw.at[n],
            recv_sem=sem_wts.at[s], device_id=(me, mate), device_id_type=MESH,
        )

    def pass_on(n, _):
        s, copy = wts_on(n)
        held(wts_r.at[s], sem_wts.at[s])
        copy.start()
        return 0

    lax.fori_loop(0, NSEC // 2, pass_on, 0)

    for h in range(2):
        held(hid_r.at[h], sem_hr.at[h])
    first = join_parts(hid_r)
    a_ref[0] = first[0:HALF]
    a_ref[1] = first[HALF:ROWS]

    lane = lanes((HALF, 128))
    lane64 = lanes((16, 128))

    def prefetch(s):
        packed = fx_r[s, 0:16].astype(F32)
        small = jnp.concatenate(
            [jnp.where((lane64 >= 32 * g) & (lane64 < 32 * g + 9), packed, 0.0) for g in range(4)],
            axis=0,
        )
        inverse = jnp.where(small > 0.0, 1.0 / jnp.where(small > 0.0, small, 1.0), 0.0)
        factor_ref[...] = dot(small.astype(BF16), spread[...])
        scale_ref[...] = dot(inverse.astype(BF16), spread[...])

    def stat_copy(s, h, j):
        target = peer_segs[j]
        return pltpu.make_async_remote_copy(
            src_ref=stat_s.at[s, h], dst_ref=stat_r.at[s, h, j - 1], send_sem=sem_st_s.at[s, h],
            recv_sem=sem_st_r.at[s, h], device_id=(target, dp), device_id_type=MESH,
        )

    def start(s, h):
        if h == 0:
            held(base_r.at[s], sem_base.at[s])

        rows = slice(HALF * h, HALF * h + HALF)
        total = jnp.zeros((HALF, 128), F32)
        for i in range(CH // 128):
            cols = slice(128 * i, 128 * i + 128)
            base = base_r[s, 2 * h : 2 * h + 2, :, cols].reshape(HALF, 128).astype(F32)
            coded = ((a_ref[h, :, cols] - base) * scale_ref[rows, cols]).astype(BF16)
            decoded = base + jnp.clip(coded.astype(F32), -448.0, 448.0) * factor_ref[rows, cols]
            d_ref[s % 2, h, :, cols] = decoded
            total = total + decoded
        own_mean = jnp.sum(total, axis=1, keepdims=True) * (1.0 / CH)
        squares = jnp.zeros((HALF, 128), F32)
        for i in range(CH // 128):
            cols = slice(128 * i, 128 * i + 128)
            center = d_ref[s % 2, h, :, cols] - own_mean
            squares = squares + center * center
            cen_ref[h, :, cols] = center.astype(BF16)
        own_m2 = jnp.sum(squares, axis=1, keepdims=True)
        pay[h, :, 0:UNITS] = dot(cen_ref[h], wts_r[s, 0:UNITS, :], NT)
        row = jnp.where(lane == 16 + chunk, own_mean, pay[h])
        row = jnp.where(lane == 24, own_m2, row)
        packed = row[0:8]
        for g in range(1, 4):
            packed = packed + pltpu.roll(row[8 * g : 8 * g + 8], 32 * g, 1)
        stat_s[s, h] = packed
        for j in range(1, NCH):
            stat_copy(s, h, j).start()

    def finish(s, h):
        up = wts_r[s, UNITS : 2 * UNITS, :]
        held(stat_r.at[s, h], sem_st_r.at[s, h])
        total = stat_s[s, h]
        for j in range(NCH - 1):
            total = total + stat_r[s, h, j]
        rows = jnp.concatenate(
            [total] + [pltpu.roll(total, 128 - 32 * g, 1) for g in range(1, 4)], axis=0
        )
        is_mean = (lane >= 16) & (lane < 24)
        mean = jnp.sum(jnp.where(is_mean, rows, 0.0), axis=1, keepdims=True) * (1.0 / NCH)
        off = jnp.where(is_mean, rows - mean, 0.0)
        squares = jnp.sum(
            jnp.where(lane == 24, rows, 0.0) + CH * off * off, axis=1, keepdims=True
        )
        rstd = lax.rsqrt(squares * (1.0 / WIDTH) + 1e-05)
        shift = dot(off.astype(BF16), fx_r[s, 16:32], NT)
        before = (rows[:, 0:UNITS] + shift) * rstd
        act = gelu(before).astype(BF16)
        added = dot(act, up)
        a_ref[h] = (d_ref[s % 2, h] + added).astype(BF16).astype(F32)
        here = slice(HALF * h, HALF * h + HALF)
        bef_ref[s, here] = before
        act_ref[s, here] = act
        mean_ref[s, here] = mean
        rstd_ref[s, here] = rstd

    def mix_copy(s, j):
        return pltpu.make_async_remote_copy(
            src_ref=mix_s.at[s, pl.ds(pl.multiple_of(8 * peer_chunks[j], 8), 8)],
            dst_ref=mix_r.at[s, j - 1], send_sem=sem_mx_s.at[s], recv_sem=sem_mx_r.at[s],
            device_id=(peer_segs[j], dp), device_id_type=MESH,
        )

    def side_work(s):
        decoded = d_ref[s % 2].reshape(ROWS, CH)
        xhat = ((decoded - mean_ref[s]) * rstd_ref[s]).astype(BF16)
        xhat_ref[s] = xhat
        mix_s[s] = dot(xhat, wuc_all[...], NT)
        for j in range(1, NCH):
            mix_copy(s, j).start()
        bpad[:, 0:UNITS] = bef_ref[s]
        bef_all[s // 8] = bef_all[s // 8] + pltpu.roll(bpad[...], 16 * (s % 8), 1)

    def weights(s, _):
        held(fx_r.at[s], sem_fx.at[s])

        @pl.when(s % 2 != z % 2)
        def _():
            held(wts_r.at[s], sem_wts.at[s])

        up = wts_r[s, UNITS : 2 * UNITS, :]
        own = pl.ds(pl.multiple_of(s * UNITS, UNITS), UNITS)
        wu_all[own, :] = up
        wuc_all[own, :] = (up.astype(F32) - fx_r[s, 16:32, 1:2].astype(F32)).astype(BF16)
        wdc_all[s] = (
            wts_r[s, 0:UNITS, :].astype(F32) - fx_r[s, 16:32, 0:1].astype(F32)
        ).astype(BF16)
        return 0

    lax.fori_loop(0, NSEC, weights, 0)

    for h in range(2):
        held(cot_r.at[h], sem_cr.at[h])
    cot = join_parts(cot_r)
    g_ref[...] = cot
    cw_s[...] = dot(cot.astype(BF16), wu_all[...], NT)

    def cw_copy(j):
        return pltpu.make_async_remote_copy(
            src_ref=cw_s.at[pl.ds(pl.multiple_of(8 * peer_chunks[j], 8), 8)],
            dst_ref=cw_r.at[j - 1],
            send_sem=sem_cw_s.at[0], recv_sem=sem_cw_r.at[0],
            device_id=(peer_segs[j], dp), device_id_type=MESH,
        )

    for j in range(1, NCH):
        cw_copy(j).start()

    products = dot(wdc_all[...].reshape(256, CH), wuc_all[...], NT)
    row_sec = lax.broadcasted_iota(jnp.int32, (256, 256), 0) // UNITS
    col_sec = lanes((256, 256)) // UNITS
    gram_s[...] = jnp.where(col_sec < row_sec, products, 0.0)
    own_gram = pl.ds(pl.multiple_of(32 * chunk, 32), 32)

    def gram_copy(j):
        return pltpu.make_async_remote_copy(
            src_ref=gram_s.at[pl.ds(pl.multiple_of(32 * peer_chunks[j], 32), 32)],
            dst_ref=gram_r.at[j - 1],
            send_sem=sem_gr_s.at[0], recv_sem=sem_gr_r.at[0],
            device_id=(peer_segs[j], dp), device_id_type=MESH,
        )

    def gm_copy(j):
        return pltpu.make_async_remote_copy(
            src_ref=gm_ref.at[own_gram], dst_ref=gm_ref.at[own_gram],
            send_sem=sem_gm_s.at[0], recv_sem=sem_gm_r.at[0],
            device_id=(peer_segs[j], dp), device_id_type=MESH,
        )

    for j in range(1, NCH):
        gram_copy(j).start()

    prefetch(0)
    for h in range(2):
        start(0, h)
    prefetch(1)

    def step(s, _):
        for h in range(2):
            finish(s, h)
            start(s + 1, h)
        side_work(s)

        @pl.when(s + 2 < NSEC)
        def _():
            prefetch(s + 2)

        @pl.when(s == 3)
        def _():
            held(gram_r, sem_gr_r.at[0])
            total = gram_s[own_gram, :]
            for j in range(NCH - 1):
                total = total + gram_r[j]
            gm_ref[own_gram, :] = total.astype(BF16)
            for j in range(1, NCH):
                gm_copy(j).start()

        return 0

    lax.fori_loop(0, NSEC - 1, step, 0)

    for h in range(2):
        finish(NSEC - 1, h)
    side_work(NSEC - 1)

    mine = pl.ds(pl.multiple_of(8 * chunk, 8), 8)

    def fold(t, _):
        held(mix_r.at[t], sem_mx_r.at[t])
        both = mix_s[t, mine, :]
        for j in range(NCH - 1):
            both = both + mix_r[t, j]
        xt_ref[t] = jnp.where(lanes((8, 256)) < UNITS * t, both, 0.0)
        return 0

    held(gm_ref.at[0 : 256 - 32], sem_gm_r.at[0])
    held(cw_r, sem_cw_r.at[0])
    grad_act = cw_s[mine, :]
    for j in range(NCH - 1):
        grad_act = grad_act + cw_r[j]
    bef8 = jnp.concatenate([bef_all[0, mine, :], bef_all[1, mine, :]], axis=1)
    slope8 = gelu_slope(bef8)
    lane8 = lanes((8, 256))
    lax.fori_loop(0, NSEC, fold, 0)

    def back(i, carry):
        grad_act, out = carry
        t = NSEC - 1 - i
        here = (lane8 >= UNITS * t) & (lane8 < UNITS * t + UNITS)
        grad_bef = jnp.where(here, grad_act * slope8, 0.0).astype(BF16)
        wide = grad_bef.astype(F32)
        c2 = jnp.sum(wide * bef8, axis=1, keepdims=True) * (1.0 / WIDTH)
        change = dot(grad_bef, gm_ref[...]) - c2 * xt_ref[t]
        return grad_act + rstd_ref[t, mine, :] * change, out + wide

    _, grad_bef = lax.fori_loop(0, NSEC, back, (grad_act, jnp.zeros((8, 256), F32)))
    gb_s[0] = grad_bef[:, 0:128]
    gb_s[1] = grad_bef[:, 128:256]

    def gb_copy(j):
        target = peer_segs[j]
        return pltpu.make_async_remote_copy(
            src_ref=gb_s, dst_ref=gb_r.at[:, mine], send_sem=sem_gb_s.at[0],
            recv_sem=sem_gb_r.at[0], device_id=(target, dp), device_id_type=MESH,
        )

    for j in range(1, NCH):
        gb_copy(j).start()
    gb_r[0, mine, :] = grad_bef[:, 0:128]
    gb_r[1, mine, :] = grad_bef[:, 128:256]
    held(gb_r.at[:, 0 : ROWS - 8], sem_gb_r.at[0])

    def x_copy(t, kind):
        to, at = (t // 2) % 2, 2 * (t // 4) + t % 2
        a, b = lax.rem(to + xh, 2), lax.rem(kind + xl, 2)
        slot = jnp.maximum(2 * a + b - 1, 0)
        return 2 * a + b, pltpu.make_async_remote_copy(
            src_ref=parts.at[to, kind, at], dst_ref=x_r.at[at, slot], send_sem=sem_xs.at[t, kind],
            recv_sem=sem_xr.at[at], device_id=(4 * y + 2 * to + core, 2 * z + kind),
            device_id_type=MESH,
        )

    def grads(i, _):
        t = NSEC - 1 - i
        to, at = (t // 2) % 2, 2 * (t // 4) + t % 2
        turned = pltpu.roll(gb_r[t // 8], lax.rem(128 - 16 * (t % 8), 128), 1)[:, 0:UNITS]
        grad_bef = turned.astype(BF16)
        g = g_ref[...]
        xhat = xhat_ref[t]
        parts[to, 0, at] = dot(grad_bef, xhat, TN).astype(BF16)
        parts[to, 1, at] = dot(act_ref[t], g.astype(BF16), TN).astype(BF16)
        for kind in range(2):
            away, copy = x_copy(t, kind)

            @pl.when(away > 0)
            def _():
                copy.start()

        c2 = jnp.sum(turned * bef_ref[t], axis=1, keepdims=True) * (1.0 / WIDTH)
        g_ref[...] = g + rstd_ref[t] * (dot(grad_bef, wdc_all[t]) - xhat.astype(F32) * c2)
        return 0

    lax.fori_loop(0, NSEC, grads, 0)

    def z_copy(i, h):
        to = 2 * i + h
        ahead = lax.rem(to - z + NZ, NZ)
        return to, pltpu.make_async_remote_copy(
            src_ref=z_s.at[i, :, 512 * h : 512 * h + 640], dst_ref=z_r.at[ahead],
            send_sem=sem_zs.at[to], recv_sem=sem_zr.at[0],
            device_id=(me, 2 * to + xl), device_id_type=MESH,
        )

    def z_send(n, _):
        i = NCH - 1 - n
        total = parts[xh, xl, i].astype(F32)
        held(x_r.at[i], sem_xr.at[i])
        for k in range(3):
            total = total + x_r[i, k].astype(F32)
        z_s[i] = total.astype(BF16)
        for h in range(2):
            to, copy = z_copy(i, h)

            @pl.when(to != z)
            def _():
                copy.start()

        return 0

    lax.fori_loop(0, NCH, z_send, 0)
    half = z % 2
    f_total = z_s[z // 2, :, pl.ds(pl.multiple_of(512 * half, 128), 640)].astype(F32)
    held(z_r.at[1:NZ], sem_zr.at[0])
    f_s[...] = lax.fori_loop(
        1, NZ, lambda n, total: total + z_r[n].astype(F32), f_total
    ).astype(BF16)

    def a_copy(to):
        return pltpu.make_async_remote_copy(
            src_ref=f_s, dst_ref=a_r.at[chunk, half], send_sem=sem_as.at[to],
            recv_sem=sem_ar.at[chunk, half], device_id=(goal, 2 * to + xl), device_id_type=MESH,
        )

    def a_send(j, _):
        to = lax.rem(z + j, NZ)

        @pl.when((goal != me) | (to != z))
        def _():
            a_copy(to).start()

        @pl.when((goal == me) & (to == z))
        def _():
            pltpu.make_async_copy(f_s, a_r.at[chunk, half], sem_ar.at[chunk, half]).start()

        return 0

    lax.fori_loop(0, NZ, a_send, 0)

    def b_copy(q, h):
        return pltpu.make_async_remote_copy(
            src_ref=a_r.at[q, h], dst_ref=b_r.at[q, h], send_sem=sem_bs.at[q, h],
            recv_sem=sem_br.at[q, h], device_id=(me, 2 * z + 1 - xl), device_id_type=MESH,
        )

    for q in range(NCH):
        for h in range(2):
            held(a_r.at[q, h], sem_ar.at[q, h])
            b_copy(q, h).start()

    for x_to in range(2):
        part_copy(x_to, hid_s, hid_r, sem_hs, sem_hr, False)
        part_copy(x_to, cot_s, cot_r, sem_cs, sem_cr, False)

    @pl.when(direct)
    def _():
        held(wts_r.at[0 : NSEC - 1], sem_ds.at[0])

    held(fx_r.at[0 : NSEC - 1], sem_ds.at[1])
    held(base_r.at[0 : NSEC - 1], sem_ds.at[2])

    def forwarded(n, _):
        wts_on(n)[1].wait_send()
        return 0

    lax.fori_loop(0, NSEC // 2, forwarded, 0)

    def left(s, _):
        for h in range(2):
            held(stat_r.at[s, h], sem_st_s.at[s, h])
        held(mix_r.at[s], sem_mx_s.at[s])
        for kind in range(2):
            away, copy = x_copy(s, kind)

            @pl.when(away > 0)
            def _():
                copy.wait_send()

        return 0

    lax.fori_loop(0, NSEC, left, 0)
    held(cw_r, sem_cw_s.at[0])
    held(gram_r, sem_gr_s.at[0])
    held(gm_ref.at[0 : 256 - 32], sem_gm_s.at[0])
    held(gb_r.at[:, 0 : ROWS - 8], sem_gb_s.at[0])

    def z_left(i, _):
        for h in range(2):
            to, copy = z_copy(i, h)

            @pl.when(to != z)
            def _():
                copy.wait_send()

        return 0

    lax.fori_loop(0, NCH, z_left, 0)

    def a_left(to, _):
        @pl.when((goal != me) | (to != z))
        def _():
            a_copy(to).wait_send()

        return 0

    lax.fori_loop(0, NZ, a_left, 0)

    for q in range(NCH):
        for h in range(2):
            b_copy(q, h).wait_recv()
            low, cols = (0, slice(CH * q, CH * q + 640)) if h == 0 else (
                128, slice(CH * q + 640, CH * q + CH))
            own, other = a_r[q, h][:, low:], b_r[q, h][:, low:]
            down = jnp.where(xl == 0, own, other)
            up_ref[:, cols] = jnp.where(xl == 0, other, own)
            down_ref[:, cols] = (down.astype(F32) * gains_ref[:, cols].astype(F32)).astype(BF16)
    for q in range(NCH):
        for h in range(2):
            b_copy(q, h).wait_send()


def whole_call(ids, hid, cot, store, exps, gains, wd, wu):
    vmem = pl.BlockSpec(memory_space=pltpu.VMEM)
    dma = pltpu.SemaphoreType.DMA

    def bf(*shape):
        return pltpu.VMEM(shape, BF16)

    def f32(*shape):
        return pltpu.VMEM(shape, F32)

    out = jax.ShapeDtypeStruct((UNITS, WIDTH), BF16)
    peers = NCH - 1
    return pl.pallas_call(
        kernel,
        name="sections",
        out_shape=(out, out),
        in_specs=[pl.BlockSpec(memory_space=pltpu.SMEM), vmem, vmem,
                  pl.BlockSpec(memory_space=pl.ANY), vmem, vmem, vmem, vmem],
        out_specs=(vmem, vmem),
        scratch_shapes=[
            bf(8, 16, 640), bf(8, 16, 640), bf(2 * UNITS, WIDTH), bf(2, NCH, 32, 128),
            bf(2, 4, 16, 640), bf(2, 4, 16, 640), bf(NSEC, 2 * UNITS, CH), bf(NSEC, 32, 128),
            bf(NSEC, 4, 16, CH),
            bf(128, CH), f32(ROWS, CH), f32(ROWS, CH), bf(256, CH), bf(256, CH),
            bf(NSEC, UNITS, CH), f32(2, HALF, CH), f32(ROWS, CH), f32(2, 2, HALF, CH),
            bf(2, HALF, CH),
            f32(2, HALF, 128), f32(ROWS, 128), f32(2, ROWS, 128), f32(NSEC, ROWS, UNITS),
            bf(NSEC, ROWS, UNITS), f32(NSEC, ROWS, 1), f32(NSEC, ROWS, 1), bf(NSEC, ROWS, CH),
            f32(NSEC, 2, 8, 128), f32(NSEC, 2, peers, 8, 128),
            f32(NSEC, ROWS, 256), f32(NSEC, peers, 8, 256),
            f32(ROWS, 256), f32(peers, 8, 256), f32(256, 256), f32(peers, 32, 256), bf(256, 256), f32(NSEC, 8, 256),
            f32(2, 8, 128), f32(2, ROWS, 128),
            bf(2, 2, NCH, UNITS, CH), bf(NCH, 3, UNITS, CH), bf(NCH, UNITS, CH),
            bf(NZ, UNITS, 640), bf(UNITS, 640), bf(NCH, 2, UNITS, 640), bf(NCH, 2, UNITS, 640),
            dma((2,)), dma((2,)), dma((2,)), dma((2,)), dma((3,)), dma((NSEC,)), dma((NSEC,)),
            dma((NSEC,)), dma((NSEC // 2,)),
            dma((NSEC, 2)), dma((NSEC, 2)), dma((NSEC,)), dma((NSEC,)), dma((1,)), dma((1,)),
            dma((1,)), dma((1,)), dma((1,)), dma((1,)), dma((1,)), dma((1,)),
            dma((NSEC, 2)), dma((NCH,)), dma((NZ,)), dma((1,)), dma((NZ,)), dma((NCH, 2)),
            dma((NCH, 2)), dma((NCH, 2)),
        ],
        compiler_params=pltpu.CompilerParams(
            collective_id=1, has_side_effects=True, vmem_limit_bytes=56 * 2**20
        ),
    )(ids, hid, cot, store, exps, gains, wd, wu)


def shards(hidden_in, cotangent, stored_bases, sample_ids, block_exps, ln_gains, w_down, w_up):
    down, up = whole_call(
        sample_ids, hidden_in, cotangent, stored_bases[0], block_exps[0], ln_gains,
        jnp.swapaxes(w_down[0], 0, 1), w_up[0],
    )
    return jnp.swapaxes(down, 0, 1)[None], up[None]


def solution(mesh):
    return jax.shard_map(
        shards,
        mesh=mesh,
        in_specs=(
            P(None, "dp", "segment"),
            P(None, "dp", "segment"),
            P("segment", None, "dp", None),
            P("dp", None),
            P("segment", None, "dp", None),
            P("segment", None),
            P("segment", None, None),
            P("segment", None, None),
        ),
        out_specs=(P("segment", None, None), P("segment", None, None)),
        check_vma=False,
    )
```

```python
import functools

import jax
import jax.numpy as jnp
from jax import lax
from jax.experimental import pallas as pl
from jax.experimental.pallas import tpu as pltpu
from jax.sharding import PartitionSpec as P

MESH = pl.DeviceIdType.MESH
F32 = jnp.float32
BF16 = jnp.bfloat16
NSEC = 16
UNITS = 16
NCH = 8
CH = 1152
WIDTH = NCH * CH
SPLIT = (slice(0, 640), slice(640, 1152))
SIZES = (640, 512)
PEERS = ((0, 0), (2, 0), (2, 1), (1, 0), (3, 0), (1, 1), (3, 1), (0, 1))
PARTNERS = (2, 4, 12, 10, 6, 14, 8, 3, 5, 13, 11, 7, 15, 9, 1)
PART = 576
NZ = 16
ROWS = 64
HALF = 32
NT = (((1,), (1,)), ((), ()))
TN = (((0,), (0,)), ((), ()))
K_GELU = 0.7978845608028654
C_GELU = 0.044715


def dot(a, b, dims=(((1,), (0,)), ((), ()))):
    return lax.dot_general(a, b, dims, preferred_element_type=F32)


def lanes(shape):
    return lax.broadcasted_iota(jnp.int32, shape, len(shape) - 1)


def gelu(x):
    return 0.5 * x * (1.0 + jnp.tanh(K_GELU * (x + C_GELU * x * x * x)))


def gelu_slope(x):
    th = jnp.tanh(K_GELU * (x + C_GELU * x * x * x))
    return 0.5 * (1.0 + th) + 0.5 * x * (1.0 - th * th) * K_GELU * (1.0 + 3.0 * C_GELU * x * x)


def power_of_two(exps):
    factor = jnp.ones(exps.shape, F32)
    for bit in range(5):
        factor = jnp.where(((-exps) >> bit) & 1 == 1, factor * F32(0.5 ** (1 << bit)), factor)
    return factor


def join_parts(ref):
    first = ref[0].reshape(ROWS, 640).astype(F32)
    second = ref[1].reshape(ROWS, 640).astype(F32)
    lane = lanes((ROWS, 128))
    turned = [pltpu.roll(second[:, 128 * i : 128 * i + 128], 64, 1) for i in range(5)]
    tiles = [first[:, 128 * i : 128 * i + 128] for i in range(4)]
    tiles.append(jnp.where(lane < 64, first[:, 512:640], turned[0]))
    for i in range(4):
        tiles.append(jnp.where(lane < 64, turned[i], turned[i + 1]))
    return jnp.concatenate(tiles, axis=1)


def held(ref, sem):
    pltpu.make_async_copy(ref, ref, sem).wait()


def kernel(
    ids_ref, hid_ref, cot_ref, store_ref, exps_ref, gains_ref, wd_ref, wu_ref,
    down_ref, up_ref,
    hid_s, cot_s, wts_s, fx_s, hid_r, cot_r, wts_r, fx_r, base_r,
    spread, factor_ref, scale_ref, wu_all, wuc_all, wdc_all, a_ref, g_ref, d_ref, cen_ref,
    pay, bpad, bef_all, bef_ref, act_ref, mean_ref, rstd_ref, xhat_ref,
    stat_s, stat_r, mix_s, mix_r, cw_s, cw_r, gram_s, gram_r, gm_ref, xt_ref, gb_s, gb_r,
    parts, x_r, z_s, z_r, f_s, a_r, b_r,
    sem_hs, sem_hr, sem_cs, sem_cr, sem_ds, sem_fx, sem_wts, sem_base, sem_fw,
    sem_st_s, sem_st_r, sem_mx_s, sem_mx_r, sem_cw_s, sem_cw_r, sem_gr_s, sem_gr_r,
    sem_gm_s, sem_gm_r, sem_gb_s, sem_gb_r,
    sem_xs, sem_xr, sem_zs, sem_zr, sem_as, sem_ar, sem_bs, sem_br,
):
    me = lax.axis_index("segment")
    dp = lax.axis_index("dp")
    y, xh, core = me // 4, (me // 2) % 2, me % 2
    z, xl = dp // 2, dp % 2
    chunk = 2 * y + core

    def seg_of(q):
        return 4 * (q // 2) + 2 * xh + q % 2

    peer_chunks = [2 * lax.rem(y + dy, 4) + lax.rem(core + dc, 2) for dy, dc in PEERS]
    peer_segs = [seg_of(q) for q in peer_chunks]
    goal = seg_of(z // 2)
    mates = [2 * lax.rem(z + step, NZ) + xl for step in (NZ - 1, 1)]

    barrier = pltpu.get_barrier_semaphore()

    def greet(device):
        pl.semaphore_signal(barrier, inc=1, device_id=device, device_id_type=MESH)

    def greet_lines(j, _):
        greet((lax.rem(me + j, NSEC), dp))
        greet((me, 2 * lax.rem(z + j, NZ) + xl))
        return 0

    lax.fori_loop(1, NSEC, greet_lines, 0)

    def x_device(a, b):
        return (4 * y + 2 * lax.rem(xh + a, 2) + core, 2 * z + lax.rem(xl + b, 2))

    for a, b in ((0, 1), (1, 0), (1, 1)):
        greet(x_device(a, b))

    def greet_goal(j, _):
        @pl.when((goal != me) | (j != z))
        def _():
            greet((goal, 2 * j + xl))

        source, at = seg_of(j // 2), 2 * chunk + j % 2

        @pl.when((source != me) | (at != z))
        def _():
            greet((source, 2 * at + xl))

        return 0

    lax.fori_loop(0, NZ, greet_goal, 0)

    hid_s[...] = jnp.zeros(hid_s.shape, BF16)
    cot_s[...] = jnp.zeros(cot_s.shape, BF16)
    lane16 = lanes((UNITS, 128))
    batches = []
    for slot in range(8):
        batch = jnp.int32(0)
        for k in range(8):
            batch = jnp.maximum(batch, jnp.where(ids_ref[0, k] == slot, k, 0))
        batches.append(batch)
        hid_s[slot, :, 0:PART] = hid_ref[batch]
        cot_s[slot, :, 0:PART] = cot_ref[batch]
    aux = jnp.zeros((UNITS, 128), F32)
    up_total = jnp.zeros((UNITS, 1), F32)
    down_total = jnp.zeros((UNITS, 1), F32)
    for q in range(NCH):
        part = slice(q * CH, (q + 1) * CH)
        scaled = (wd_ref[:, part].astype(F32) * gains_ref[:, part].astype(F32)).astype(BF16)
        wts_s[0:UNITS, part] = scaled
        up = wu_ref[:, part]
        wts_s[UNITS : 2 * UNITS, part] = up
        down_sum = jnp.sum(scaled.astype(F32), axis=1, keepdims=True)
        aux = aux + jnp.where(lane16 == 16 + q, down_sum, 0.0)
        down_total = down_total + down_sum
        up_total = up_total + jnp.sum(up.astype(F32), axis=1, keepdims=True)
    aux = aux + jnp.where(lane16 == 0, down_total * (1.0 / WIDTH), 0.0)
    aux = (aux + jnp.where(lane16 == 1, up_total * (1.0 / WIDTH), 0.0)).astype(BF16)
    bpad[...] = jnp.zeros(bpad.shape, F32)
    for x_to in range(2):
        picks = []
        for g in range(4):
            bpad[0:16, 0:72] = power_of_two(exps_ref[batches[4 * x_to + g]])
            picks.append(bpad[0:16, :])
        for q in range(NCH):
            packed = jnp.zeros((16, 128), F32)
            for g in range(4):
                turned = pltpu.roll(picks[g], (32 * g - 9 * q) % 128, 1)
                packed = jnp.where((lane16 >= 32 * g) & (lane16 < 32 * g + 9), turned, packed)
            fx_s[x_to, q, 0:16] = packed.astype(BF16)
            fx_s[x_to, q, 16:32] = aux

    pl.semaphore_wait(
        barrier, 2 * (NSEC - 1) + 3 + 2 * NZ - 2 * jnp.where(goal == me, 1, 0)
    )

    def part_copy(x_to, src, dst, send, recv, go):
        target = 4 * y + 2 * x_to + xh
        rows = src.at[4 * x_to : 4 * x_to + 4]

        if go:

            @pl.when(target == me)
            def _():
                pltpu.make_async_copy(rows, dst.at[core], recv.at[core]).start()

        @pl.when(target != me)
        def _():
            copy = pltpu.make_async_remote_copy(
                src_ref=rows, dst_ref=dst.at[core], send_sem=send.at[x_to],
                recv_sem=recv.at[core], device_id=(target, dp), device_id_type=MESH,
            )
            copy.start() if go else copy.wait_send()

    for x_to in range(2):
        part_copy(x_to, hid_s, hid_r, sem_hs, sem_hr, True)

    def place(target):
        to_chunk = 2 * (target // 4) + target % 2
        return (target // 2) % 2, to_chunk, pl.ds(pl.multiple_of(to_chunk * CH, 128), CH)

    def data_send(kind):
        def pair(target):
            x_to, to_chunk, cols = place(target)
            if kind == 0:
                return wts_s.at[:, cols], wts_r.at[me], sem_wts.at[me]
            if kind == 1:
                return fx_s.at[x_to, to_chunk], fx_r.at[me], sem_fx.at[me]
            return store_ref.at[pl.ds(4 * x_to, 4), :, cols], base_r.at[me], sem_base.at[me]

        src, dst, sem = pair(me)
        pltpu.make_async_copy(src, dst, sem).start()
        for bits in PARTNERS:
            target = me ^ bits
            src, dst, sem = pair(target)
            pltpu.make_async_remote_copy(
                src_ref=src, dst_ref=dst, send_sem=sem_ds.at[kind], recv_sem=sem,
                device_id=(target, dp), device_id_type=MESH,
            ).start()

    def wts_on(n, k):
        s = 2 * n + z % 2
        part = pl.ds(k * UNITS, UNITS)
        return pltpu.make_async_remote_copy(
            src_ref=wts_r.at[s, part], dst_ref=wts_r.at[s, part], send_sem=sem_fw.at[n],
            recv_sem=sem_wts.at[s], device_id=(me, mates[k]), device_id_type=MESH,
        )

    def pass_on(n, _):
        s = 2 * n + z % 2
        held(wts_r.at[s], sem_wts.at[s])
        for k in range(2):
            wts_on(n, k).start()
        return 0

    direct = core == z % 2

    @pl.when(direct)
    def _():
        data_send(0)

    data_send(1)
    data_send(2)
    lax.fori_loop(0, NSEC // 2, pass_on, 0)
    for x_to in range(2):
        part_copy(x_to, cot_s, cot_r, sem_cs, sem_cr, True)

    block = lax.broadcasted_iota(jnp.int32, (128, CH), 0)
    feature = lax.broadcasted_iota(jnp.int32, (128, CH), 1)
    spread[...] = jnp.where((block & 31) == (feature >> 7), 1.0, 0.0).astype(BF16)
    pay[...] = jnp.zeros(pay.shape, F32)
    bpad[...] = jnp.zeros(bpad.shape, F32)
    bef_all[...] = jnp.zeros(bef_all.shape, F32)

    for h in range(2):
        held(hid_r.at[h], sem_hr.at[h])
    first = join_parts(hid_r)
    a_ref[0] = first[0:HALF]
    a_ref[1] = first[HALF:ROWS]

    lane = lanes((HALF, 128))
    lane64 = lanes((16, 128))

    def prefetch(s):
        packed = fx_r[s, 0:16].astype(F32)
        small = jnp.concatenate(
            [jnp.where((lane64 >= 32 * g) & (lane64 < 32 * g + 9), packed, 0.0) for g in range(4)],
            axis=0,
        )
        inverse = jnp.where(small > 0.0, 1.0 / jnp.where(small > 0.0, small, 1.0), 0.0)
        factor_ref[...] = dot(small.astype(BF16), spread[...])
        scale_ref[...] = dot(inverse.astype(BF16), spread[...])

    def stat_copy(s, h, j):
        target = peer_segs[j]
        return pltpu.make_async_remote_copy(
            src_ref=stat_s.at[s, h], dst_ref=stat_r.at[s, h, j - 1], send_sem=sem_st_s.at[s, h],
            recv_sem=sem_st_r.at[s, h], device_id=(target, dp), device_id_type=MESH,
        )

    def start(s, h):
        if h == 0:
            held(base_r.at[s], sem_base.at[s])

        rows = slice(HALF * h, HALF * h + HALF)
        total = jnp.zeros((HALF, 128), F32)
        for i in range(CH // 128):
            cols = slice(128 * i, 128 * i + 128)
            base = base_r[s, 2 * h : 2 * h + 2, :, cols].reshape(HALF, 128).astype(F32)
            coded = ((a_ref[h, :, cols] - base) * scale_ref[rows, cols]).astype(BF16)
            decoded = base + jnp.clip(coded.astype(F32), -448.0, 448.0) * factor_ref[rows, cols]
            d_ref[s % 2, h, :, cols] = decoded
            total = total + decoded
        own_mean = jnp.sum(total, axis=1, keepdims=True) * (1.0 / CH)
        squares = jnp.zeros((HALF, 128), F32)
        for i in range(CH // 128):
            cols = slice(128 * i, 128 * i + 128)
            center = d_ref[s % 2, h, :, cols] - own_mean
            squares = squares + center * center
            cen_ref[h, :, cols] = center.astype(BF16)
        own_m2 = jnp.sum(squares, axis=1, keepdims=True)
        pay[h, :, 0:UNITS] = dot(cen_ref[h], wts_r[s, 0:UNITS, :], NT)
        row = jnp.where(lane == 16 + chunk, own_mean, pay[h])
        row = jnp.where(lane == 24, own_m2, row)
        packed = row[0:8]
        for g in range(1, 4):
            packed = packed + pltpu.roll(row[8 * g : 8 * g + 8], 32 * g, 1)
        stat_s[s, h] = packed
        for j in range(1, NCH):
            stat_copy(s, h, j).start()

    def finish(s, h):
        up = wts_r[s, UNITS : 2 * UNITS, :]
        held(stat_r.at[s, h], sem_st_r.at[s, h])
        total = stat_s[s, h]
        for j in range(NCH - 1):
            total = total + stat_r[s, h, j]
        rows = jnp.concatenate(
            [total] + [pltpu.roll(total, 128 - 32 * g, 1) for g in range(1, 4)], axis=0
        )
        is_mean = (lane >= 16) & (lane < 24)
        mean = jnp.sum(jnp.where(is_mean, rows, 0.0), axis=1, keepdims=True) * (1.0 / NCH)
        off = jnp.where(is_mean, rows - mean, 0.0)
        squares = jnp.sum(
            jnp.where(lane == 24, rows, 0.0) + CH * off * off, axis=1, keepdims=True
        )
        rstd = lax.rsqrt(squares * (1.0 / WIDTH) + 1e-05)
        shift = dot(off.astype(BF16), fx_r[s, 16:32], NT)
        before = (rows[:, 0:UNITS] + shift) * rstd
        act = gelu(before).astype(BF16)
        added = dot(act, up)
        a_ref[h] = (d_ref[s % 2, h] + added).astype(BF16).astype(F32)
        here = slice(HALF * h, HALF * h + HALF)
        bef_ref[s, here] = before
        act_ref[s, here] = act
        mean_ref[s, here] = mean
        rstd_ref[s, here] = rstd

    def mix_copy(s, j):
        return pltpu.make_async_remote_copy(
            src_ref=mix_s.at[s, pl.ds(pl.multiple_of(8 * peer_chunks[j], 8), 8)],
            dst_ref=mix_r.at[s, j - 1], send_sem=sem_mx_s.at[s], recv_sem=sem_mx_r.at[s],
            device_id=(peer_segs[j], dp), device_id_type=MESH,
        )

    def side_work(s):
        decoded = d_ref[s % 2].reshape(ROWS, CH)
        xhat = ((decoded - mean_ref[s]) * rstd_ref[s]).astype(BF16)
        xhat_ref[s] = xhat
        mix_s[s] = dot(xhat, wuc_all[...], NT)
        for j in range(1, NCH):
            mix_copy(s, j).start()
        bpad[:, 0:UNITS] = bef_ref[s]
        bef_all[s // 8] = bef_all[s // 8] + pltpu.roll(bpad[...], 16 * (s % 8), 1)

    def weights(s, _):
        held(fx_r.at[s], sem_fx.at[s])

        @pl.when(s % 2 != z % 2)
        def _():
            held(wts_r.at[s], sem_wts.at[s])

        up = wts_r[s, UNITS : 2 * UNITS, :]
        own = pl.ds(pl.multiple_of(s * UNITS, UNITS), UNITS)
        wu_all[own, :] = up
        wuc_all[own, :] = (up.astype(F32) - fx_r[s, 16:32, 1:2].astype(F32)).astype(BF16)
        wdc_all[s] = (
            wts_r[s, 0:UNITS, :].astype(F32) - fx_r[s, 16:32, 0:1].astype(F32)
        ).astype(BF16)
        return 0

    lax.fori_loop(0, NSEC, weights, 0)

    def cw_copy(j):
        return pltpu.make_async_remote_copy(
            src_ref=cw_s.at[pl.ds(pl.multiple_of(8 * peer_chunks[j], 8), 8)],
            dst_ref=cw_r.at[j - 1],
            send_sem=sem_cw_s.at[0], recv_sem=sem_cw_r.at[0],
            device_id=(peer_segs[j], dp), device_id_type=MESH,
        )

    def cotangent_products():
        for h in range(2):
            held(cot_r.at[h], sem_cr.at[h])
        cot = join_parts(cot_r)
        g_ref[...] = cot
        cw_s[...] = dot(cot.astype(BF16), wu_all[...], NT)
        for j in range(1, NCH):
            cw_copy(j).start()

    own_gram = pl.ds(pl.multiple_of(32 * chunk, 32), 32)

    def gram_copy(j):
        return pltpu.make_async_remote_copy(
            src_ref=gram_s.at[pl.ds(pl.multiple_of(32 * peer_chunks[j], 32), 32)],
            dst_ref=gram_r.at[j - 1],
            send_sem=sem_gr_s.at[0], recv_sem=sem_gr_r.at[0],
            device_id=(peer_segs[j], dp), device_id_type=MESH,
        )

    def gm_copy(j):
        return pltpu.make_async_remote_copy(
            src_ref=gm_ref.at[own_gram], dst_ref=gm_ref.at[own_gram],
            send_sem=sem_gm_s.at[0], recv_sem=sem_gm_r.at[0],
            device_id=(peer_segs[j], dp), device_id_type=MESH,
        )

    def gram_products():
        products = dot(wdc_all[...].reshape(256, CH), wuc_all[...], NT)
        row_sec = lax.broadcasted_iota(jnp.int32, (256, 256), 0) >> 4
        col_sec = lanes((256, 256)) >> 4
        gram_s[...] = jnp.where(col_sec < row_sec, products, 0.0)
        for j in range(1, NCH):
            gram_copy(j).start()

    prefetch(0)
    for h in range(2):
        start(0, h)
    prefetch(1)

    def step(s, _):
        for h in range(2):
            finish(s, h)
            start(s + 1, h)
        side_work(s)

        @pl.when(s + 2 < NSEC)
        def _():
            prefetch(s + 2)

        @pl.when(s == 1)
        def _():
            cotangent_products()

        @pl.when(s == 3)
        def _():
            gram_products()

        @pl.when(s == 6)
        def _():
            held(gram_r, sem_gr_r.at[0])
            total = gram_s[own_gram, :]
            for j in range(NCH - 1):
                total = total + gram_r[j]
            gm_ref[own_gram, :] = total.astype(BF16)
            for j in range(1, NCH):
                gm_copy(j).start()

        return 0

    lax.fori_loop(0, NSEC - 1, step, 0)

    for h in range(2):
        finish(NSEC - 1, h)
    side_work(NSEC - 1)

    mine = pl.ds(pl.multiple_of(8 * chunk, 8), 8)

    def fold(t, _):
        held(mix_r.at[t], sem_mx_r.at[t])
        both = mix_s[t, mine, :]
        for j in range(NCH - 1):
            both = both + mix_r[t, j]
        xt_ref[t] = jnp.where(lanes((8, 256)) < UNITS * t, both, 0.0)
        return 0

    held(gm_ref.at[0 : 256 - 32], sem_gm_r.at[0])
    held(cw_r, sem_cw_r.at[0])
    grad_act = cw_s[mine, :]
    for j in range(NCH - 1):
        grad_act = grad_act + cw_r[j]
    bef8 = jnp.concatenate([bef_all[0, mine, :], bef_all[1, mine, :]], axis=1)
    slope8 = gelu_slope(bef8)
    lane8 = lanes((8, 256))
    lax.fori_loop(0, NSEC, fold, 0)

    def back(i, carry):
        grad_act, out = carry
        t = NSEC - 1 - i
        here = (lane8 >= UNITS * t) & (lane8 < UNITS * t + UNITS)
        grad_bef = jnp.where(here, grad_act * slope8, 0.0).astype(BF16)
        wide = grad_bef.astype(F32)
        c2 = jnp.sum(wide * bef8, axis=1, keepdims=True) * (1.0 / WIDTH)
        change = dot(grad_bef, gm_ref[...]) - c2 * xt_ref[t]
        return grad_act + rstd_ref[t, mine, :] * change, out + wide

    _, grad_bef = lax.fori_loop(0, NSEC, back, (grad_act, jnp.zeros((8, 256), F32)))
    gb_s[0] = grad_bef[:, 0:128]
    gb_s[1] = grad_bef[:, 128:256]

    def gb_copy(j):
        target = peer_segs[j]
        return pltpu.make_async_remote_copy(
            src_ref=gb_s, dst_ref=gb_r.at[:, mine], send_sem=sem_gb_s.at[0],
            recv_sem=sem_gb_r.at[0], device_id=(target, dp), device_id_type=MESH,
        )

    for j in range(1, NCH):
        gb_copy(j).start()
    gb_r[0, mine, :] = grad_bef[:, 0:128]
    gb_r[1, mine, :] = grad_bef[:, 128:256]
    held(gb_r.at[:, 0 : ROWS - 8], sem_gb_r.at[0])

    def x_copy(t, kind):
        to, at = (t // 2) % 2, 2 * (t // 4) + t % 2
        a, b = lax.rem(to + xh, 2), lax.rem(kind + xl, 2)
        slot = jnp.maximum(2 * a + b - 1, 0)
        return 2 * a + b, pltpu.make_async_remote_copy(
            src_ref=parts.at[to, kind, at], dst_ref=x_r.at[at, slot], send_sem=sem_xs.at[t, kind],
            recv_sem=sem_xr.at[at], device_id=(4 * y + 2 * to + core, 2 * z + kind),
            device_id_type=MESH,
        )

    def grads(i, _):
        t = NSEC - 1 - i
        to, at = (t // 2) % 2, 2 * (t // 4) + t % 2
        turned = pltpu.roll(gb_r[t // 8], lax.rem(128 - 16 * (t % 8), 128), 1)[:, 0:UNITS]
        grad_bef = turned.astype(BF16)
        g = g_ref[...]
        xhat = xhat_ref[t]
        parts[to, 0, at] = dot(grad_bef, xhat, TN).astype(BF16)
        parts[to, 1, at] = dot(act_ref[t], g.astype(BF16), TN).astype(BF16)
        for kind in range(2):
            away, copy = x_copy(t, kind)

            @pl.when(away > 0)
            def _():
                copy.start()

        c2 = jnp.sum(turned * bef_ref[t], axis=1, keepdims=True) * (1.0 / WIDTH)
        g_ref[...] = g + rstd_ref[t] * (dot(grad_bef, wdc_all[t]) - xhat.astype(F32) * c2)
        return 0

    lax.fori_loop(0, NSEC, grads, 0)

    def z_copy(i, h):
        to = 2 * i + h
        ahead = lax.rem(to - z + NZ, NZ)
        return to, pltpu.make_async_remote_copy(
            src_ref=z_s.at[i, :, SPLIT[h]], dst_ref=z_r.at[ahead, :, 0 : SIZES[h]],
            send_sem=sem_zs.at[to], recv_sem=sem_zr.at[0],
            device_id=(me, 2 * to + xl), device_id_type=MESH,
        )

    def z_send(n, _):
        i = NCH - 1 - n
        total = parts[xh, xl, i].astype(F32)
        held(x_r.at[i], sem_xr.at[i])
        for k in range(3):
            total = total + x_r[i, k].astype(F32)
        z_s[i] = total.astype(BF16)
        for h in range(2):
            to, copy = z_copy(i, h)

            @pl.when(to != z)
            def _():
                copy.start()

        return 0

    lax.fori_loop(0, NCH, z_send, 0)
    half = z % 2
    f_total = jnp.concatenate(
        [z_s[z // 2, :, pl.ds(pl.multiple_of(640 * half, 128), 512)], z_s[z // 2, :, 512:640]],
        axis=1,
    ).astype(F32)
    for h in range(2):

        @pl.when(half == h)
        def _():
            held(z_r.at[1:NZ, :, 0 : SIZES[h]], sem_zr.at[0])

    f_s[...] = lax.fori_loop(
        1, NZ, lambda n, total: total + z_r[n].astype(F32), f_total
    ).astype(BF16)

    def a_copy(to, h):
        return pltpu.make_async_remote_copy(
            src_ref=f_s.at[:, 0 : SIZES[h]], dst_ref=a_r.at[chunk, h, :, 0 : SIZES[h]],
            send_sem=sem_as.at[to], recv_sem=sem_ar.at[chunk, h],
            device_id=(goal, 2 * to + xl), device_id_type=MESH,
        )

    def a_send(j, _):
        to = lax.rem(z + j, NZ)
        here = (goal == me) & (to == z)
        for h in range(2):

            @pl.when(jnp.logical_not(here) & (half == h))
            def _():
                a_copy(to, h).start()

            @pl.when(here & (half == h))
            def _():
                pltpu.make_async_copy(
                    f_s.at[:, 0 : SIZES[h]], a_r.at[chunk, h, :, 0 : SIZES[h]],
                    sem_ar.at[chunk, h],
                ).start()

        return 0

    lax.fori_loop(0, NZ, a_send, 0)

    def b_copy(q, h):
        return pltpu.make_async_remote_copy(
            src_ref=a_r.at[q, h, :, 0 : SIZES[h]], dst_ref=b_r.at[q, h, :, 0 : SIZES[h]],
            send_sem=sem_bs.at[q, h],
            recv_sem=sem_br.at[q, h], device_id=(me, 2 * z + 1 - xl), device_id_type=MESH,
        )

    for q in range(NCH):
        for h in range(2):
            held(a_r.at[q, h, :, 0 : SIZES[h]], sem_ar.at[q, h])
            b_copy(q, h).start()

    for x_to in range(2):
        part_copy(x_to, hid_s, hid_r, sem_hs, sem_hr, False)
        part_copy(x_to, cot_s, cot_r, sem_cs, sem_cr, False)

    @pl.when(direct)
    def _():
        held(wts_r.at[0 : NSEC - 1], sem_ds.at[0])

    held(fx_r.at[0 : NSEC - 1], sem_ds.at[1])
    held(base_r.at[0 : NSEC - 1], sem_ds.at[2])

    def forwarded(n, _):
        held(wts_r.at[0], sem_fw.at[n])
        return 0

    lax.fori_loop(0, NSEC // 2, forwarded, 0)

    def left(s, _):
        for h in range(2):
            held(stat_r.at[s, h], sem_st_s.at[s, h])
        held(mix_r.at[s], sem_mx_s.at[s])
        for kind in range(2):
            away, copy = x_copy(s, kind)

            @pl.when(away > 0)
            def _():
                copy.wait_send()

        return 0

    lax.fori_loop(0, NSEC, left, 0)
    held(cw_r, sem_cw_s.at[0])
    held(gram_r, sem_gr_s.at[0])
    held(gm_ref.at[0 : 256 - 32], sem_gm_s.at[0])
    held(gb_r.at[:, 0 : ROWS - 8], sem_gb_s.at[0])

    def z_left(i, _):
        for h in range(2):
            to, copy = z_copy(i, h)

            @pl.when(to != z)
            def _():
                copy.wait_send()

        return 0

    lax.fori_loop(0, NCH, z_left, 0)

    def a_left(to, _):
        for h in range(2):

            @pl.when(((goal != me) | (to != z)) & (half == h))
            def _():
                a_copy(to, h).wait_send()

        return 0

    lax.fori_loop(0, NZ, a_left, 0)

    for q in range(NCH):
        for h in range(2):
            b_copy(q, h).wait_recv()
            cols = slice(CH * q + SPLIT[h].start, CH * q + SPLIT[h].stop)
            own, other = a_r[q, h, :, 0 : SIZES[h]], b_r[q, h, :, 0 : SIZES[h]]
            down = jnp.where(xl == 0, own, other)
            up_ref[:, cols] = jnp.where(xl == 0, other, own)
            down_ref[:, cols] = (down.astype(F32) * gains_ref[:, cols].astype(F32)).astype(BF16)
    for q in range(NCH):
        for h in range(2):
            b_copy(q, h).wait_send()


def whole_call(ids, hid, cot, store, exps, gains, wd, wu):
    vmem = pl.BlockSpec(memory_space=pltpu.VMEM)
    dma = pltpu.SemaphoreType.DMA

    def bf(*shape):
        return pltpu.VMEM(shape, BF16)

    def f32(*shape):
        return pltpu.VMEM(shape, F32)

    out = jax.ShapeDtypeStruct((UNITS, WIDTH), BF16)
    peers = NCH - 1
    return pl.pallas_call(
        kernel,
        name="sections",
        out_shape=(out, out),
        in_specs=[pl.BlockSpec(memory_space=pltpu.SMEM), vmem, vmem,
                  pl.BlockSpec(memory_space=pl.ANY), vmem, vmem, vmem, vmem],
        out_specs=(vmem, vmem),
        scratch_shapes=[
            bf(8, 16, 640), bf(8, 16, 640), bf(2 * UNITS, WIDTH), bf(2, NCH, 32, 128),
            bf(2, 4, 16, 640), bf(2, 4, 16, 640), bf(NSEC, 2 * UNITS, CH), bf(NSEC, 32, 128),
            bf(NSEC, 4, 16, CH),
            bf(128, CH), f32(ROWS, CH), f32(ROWS, CH), bf(256, CH), bf(256, CH),
            bf(NSEC, UNITS, CH), f32(2, HALF, CH), f32(ROWS, CH), f32(2, 2, HALF, CH),
            bf(2, HALF, CH),
            f32(2, HALF, 128), f32(ROWS, 128), f32(2, ROWS, 128), f32(NSEC, ROWS, UNITS),
            bf(NSEC, ROWS, UNITS), f32(NSEC, ROWS, 1), f32(NSEC, ROWS, 1), bf(NSEC, ROWS, CH),
            f32(NSEC, 2, 8, 128), f32(NSEC, 2, peers, 8, 128),
            f32(NSEC, ROWS, 256), f32(NSEC, peers, 8, 256),
            f32(ROWS, 256), f32(peers, 8, 256), f32(256, 256), f32(peers, 32, 256), bf(256, 256), f32(NSEC, 8, 256),
            f32(2, 8, 128), f32(2, ROWS, 128),
            bf(2, 2, NCH, UNITS, CH), bf(NCH, 3, UNITS, CH), bf(NCH, UNITS, CH),
            bf(NZ, UNITS, 640), bf(UNITS, 640), bf(NCH, 2, UNITS, 640), bf(NCH, 2, UNITS, 640),
            dma((2,)), dma((2,)), dma((2,)), dma((2,)), dma((3,)), dma((NSEC,)), dma((NSEC,)),
            dma((NSEC,)), dma((NSEC // 2,)),
            dma((NSEC, 2)), dma((NSEC, 2)), dma((NSEC,)), dma((NSEC,)), dma((1,)), dma((1,)),
            dma((1,)), dma((1,)), dma((1,)), dma((1,)), dma((1,)), dma((1,)),
            dma((NSEC, 2)), dma((NCH,)), dma((NZ,)), dma((1,)), dma((NZ,)), dma((NCH, 2)),
            dma((NCH, 2)), dma((NCH, 2)),
        ],
        compiler_params=pltpu.CompilerParams(
            collective_id=1, has_side_effects=True, vmem_limit_bytes=56 * 2**20
        ),
    )(ids, hid, cot, store, exps, gains, wd, wu)


def shards(hidden_in, cotangent, stored_bases, sample_ids, block_exps, ln_gains, w_down, w_up):
    down, up = whole_call(
        sample_ids, hidden_in, cotangent, stored_bases[0], block_exps[0], ln_gains,
        jnp.swapaxes(w_down[0], 0, 1), w_up[0],
    )
    return jnp.swapaxes(down, 0, 1)[None], up[None]


def solution(mesh):
    return jax.shard_map(
        shards,
        mesh=mesh,
        in_specs=(
            P(None, "dp", "segment"),
            P(None, "dp", "segment"),
            P("segment", None, "dp", None),
            P("dp", None),
            P("segment", None, "dp", None),
            P("segment", None),
            P("segment", None, None),
            P("segment", None, None),
        ),
        out_specs=(P("segment", None, None), P("segment", None, None)),
        check_vma=False,
    )
```

```python
import functools

import jax
import jax.numpy as jnp
from jax import lax
from jax.experimental import pallas as pl
from jax.experimental.pallas import tpu as pltpu
from jax.sharding import PartitionSpec as P

MESH = pl.DeviceIdType.MESH
F32 = jnp.float32
BF16 = jnp.bfloat16
NSEC = 16
UNITS = 16
NCH = 8
CH = 1152
WIDTH = NCH * CH
SPLIT = (slice(0, 640), slice(640, 1152))
SIZES = (640, 512)
PEERS = ((0, 0), (2, 0), (2, 1), (1, 0), (3, 0), (1, 1), (3, 1), (0, 1))
PARTNERS = (2, 4, 12, 10, 6, 14, 8, 3, 5, 13, 11, 7, 15, 9, 1)
PART = 576
NZ = 16
ROWS = 64
HALF = 32
NT = (((1,), (1,)), ((), ()))
TN = (((0,), (0,)), ((), ()))
K_GELU = 0.7978845608028654
C_GELU = 0.044715


def dot(a, b, dims=(((1,), (0,)), ((), ()))):
    return lax.dot_general(a, b, dims, preferred_element_type=F32)


def lanes(shape):
    return lax.broadcasted_iota(jnp.int32, shape, len(shape) - 1)


def gelu(x):
    return 0.5 * x * (1.0 + jnp.tanh(K_GELU * (x + C_GELU * x * x * x)))


def gelu_slope(x):
    th = jnp.tanh(K_GELU * (x + C_GELU * x * x * x))
    return 0.5 * (1.0 + th) + 0.5 * x * (1.0 - th * th) * K_GELU * (1.0 + 3.0 * C_GELU * x * x)


def power_of_two(exps):
    factor = jnp.ones(exps.shape, F32)
    for bit in range(5):
        factor = jnp.where(((-exps) >> bit) & 1 == 1, factor * F32(0.5 ** (1 << bit)), factor)
    return factor


def join_parts(ref):
    first = ref[0].reshape(ROWS, 640).astype(F32)
    second = ref[1].reshape(ROWS, 640).astype(F32)
    lane = lanes((ROWS, 128))
    turned = [pltpu.roll(second[:, 128 * i : 128 * i + 128], 64, 1) for i in range(5)]
    tiles = [first[:, 128 * i : 128 * i + 128] for i in range(4)]
    tiles.append(jnp.where(lane < 64, first[:, 512:640], turned[0]))
    for i in range(4):
        tiles.append(jnp.where(lane < 64, turned[i], turned[i + 1]))
    return jnp.concatenate(tiles, axis=1)


def held(ref, sem):
    pltpu.make_async_copy(ref, ref, sem).wait()


def kernel(
    ids_ref, hid_ref, cot_ref, store_ref, exps_ref, gains_ref, wd_ref, wu_ref,
    down_ref, up_ref,
    hid_s, cot_s, wts_s, fx_s, hid_r, cot_r, wts_r, fx_r, base_r,
    spread, factor_ref, scale_ref, wu_all, wuc_all, wdc_all, a_ref, g_ref, d_ref, cen_ref,
    pay, bpad, bef_all, bef_ref, act_ref, mean_ref, rstd_ref, xhat_ref,
    stat_s, stat_r, mix_s, mix_r, cw_s, cw_r, gram_s, gram_r, gm_ref, xt_ref, gb_s, gb_r,
    parts, x_r, z_s, z_r, f_s, a_r, b_r,
    sem_hs, sem_hr, sem_cs, sem_cr, sem_ds, sem_fx, sem_wts, sem_base, sem_fw,
    sem_st_s, sem_st_r, sem_mx_s, sem_mx_r, sem_cw_s, sem_cw_r, sem_gr_s, sem_gr_r,
    sem_gm_s, sem_gm_r, sem_gb_s, sem_gb_r,
    sem_xs, sem_xr, sem_zs, sem_zr, sem_as, sem_ar, sem_bs, sem_br,
):
    me = lax.axis_index("segment")
    dp = lax.axis_index("dp")
    y, xh, core = me // 4, (me // 2) % 2, me % 2
    z, xl = dp // 2, dp % 2
    chunk = 2 * y + core

    def seg_of(q):
        return 4 * (q // 2) + 2 * xh + q % 2

    peer_chunks = [2 * lax.rem(y + dy, 4) + lax.rem(core + dc, 2) for dy, dc in PEERS]
    peer_segs = [seg_of(q) for q in peer_chunks]
    pick, half = lax.rem(z % NCH + 4 * core, NCH), z // NCH
    goal = seg_of(pick)
    mates = [2 * lax.rem(z + step, NZ) + xl for step in (NZ - 1, 1)]

    barrier = pltpu.get_barrier_semaphore()

    def greet(device):
        pl.semaphore_signal(barrier, inc=1, device_id=device, device_id_type=MESH)

    def greet_lines(j, _):
        greet((lax.rem(me + j, NSEC), dp))
        greet((me, 2 * lax.rem(z + j, NZ) + xl))
        return 0

    lax.fori_loop(1, NSEC, greet_lines, 0)

    def x_device(a, b):
        return (4 * y + 2 * lax.rem(xh + a, 2) + core, 2 * z + lax.rem(xl + b, 2))

    for a, b in ((0, 1), (1, 0), (1, 1)):
        greet(x_device(a, b))

    def greet_goal(j, _):
        @pl.when((goal != me) | (j != z))
        def _():
            greet((goal, 2 * j + xl))

        source, at = seg_of(j // 2), lax.rem(chunk + 4 * ((j // 2) % 2), NCH) + NCH * (j % 2)

        @pl.when((source != me) | (at != z))
        def _():
            greet((source, 2 * at + xl))

        return 0

    lax.fori_loop(0, NZ, greet_goal, 0)

    hid_s[...] = jnp.zeros(hid_s.shape, BF16)
    cot_s[...] = jnp.zeros(cot_s.shape, BF16)
    lane16 = lanes((UNITS, 128))
    batches = []
    for slot in range(8):
        batch = jnp.int32(0)
        for k in range(8):
            batch = jnp.maximum(batch, jnp.where(ids_ref[0, k] == slot, k, 0))
        batches.append(batch)
        hid_s[slot, :, 0:PART] = hid_ref[batch]
        cot_s[slot, :, 0:PART] = cot_ref[batch]
    aux = jnp.zeros((UNITS, 128), F32)
    up_total = jnp.zeros((UNITS, 1), F32)
    down_total = jnp.zeros((UNITS, 1), F32)
    for q in range(NCH):
        part = slice(q * CH, (q + 1) * CH)
        scaled = (wd_ref[:, part].astype(F32) * gains_ref[:, part].astype(F32)).astype(BF16)
        wts_s[0:UNITS, part] = scaled
        up = wu_ref[:, part]
        wts_s[UNITS : 2 * UNITS, part] = up
        down_sum = jnp.sum(scaled.astype(F32), axis=1, keepdims=True)
        aux = aux + jnp.where(lane16 == 16 + q, down_sum, 0.0)
        down_total = down_total + down_sum
        up_total = up_total + jnp.sum(up.astype(F32), axis=1, keepdims=True)
    aux = aux + jnp.where(lane16 == 0, down_total * (1.0 / WIDTH), 0.0)
    aux = (aux + jnp.where(lane16 == 1, up_total * (1.0 / WIDTH), 0.0)).astype(BF16)
    bpad[...] = jnp.zeros(bpad.shape, F32)
    for x_to in range(2):
        picks = []
        for g in range(4):
            bpad[0:16, 0:72] = power_of_two(exps_ref[batches[4 * x_to + g]])
            picks.append(bpad[0:16, :])
        for q in range(NCH):
            packed = jnp.zeros((16, 128), F32)
            for g in range(4):
                turned = pltpu.roll(picks[g], (32 * g - 9 * q) % 128, 1)
                packed = jnp.where((lane16 >= 32 * g) & (lane16 < 32 * g + 9), turned, packed)
            fx_s[x_to, q, 0:16] = packed.astype(BF16)
            fx_s[x_to, q, 16:32] = aux

    pl.semaphore_wait(
        barrier, 2 * (NSEC - 1) + 3 + 2 * NZ - 2 * jnp.where(goal == me, 1, 0)
    )

    def part_copy(x_to, src, dst, send, recv, go):
        target = 4 * y + 2 * x_to + xh
        rows = src.at[4 * x_to : 4 * x_to + 4]

        if go:

            @pl.when(target == me)
            def _():
                pltpu.make_async_copy(rows, dst.at[core], recv.at[core]).start()

        @pl.when(target != me)
        def _():
            copy = pltpu.make_async_remote_copy(
                src_ref=rows, dst_ref=dst.at[core], send_sem=send.at[x_to],
                recv_sem=recv.at[core], device_id=(target, dp), device_id_type=MESH,
            )
            copy.start() if go else copy.wait_send()

    for x_to in range(2):
        part_copy(x_to, hid_s, hid_r, sem_hs, sem_hr, True)

    def place(target):
        to_chunk = 2 * (target // 4) + target % 2
        return (target // 2) % 2, to_chunk, pl.ds(pl.multiple_of(to_chunk * CH, 128), CH)

    def data_send(kind):
        def pair(target):
            x_to, to_chunk, cols = place(target)
            if kind == 0:
                return wts_s.at[:, cols], wts_r.at[me], sem_wts.at[me]
            if kind == 1:
                return fx_s.at[x_to, to_chunk], fx_r.at[me], sem_fx.at[me]
            return store_ref.at[pl.ds(4 * x_to, 4), :, cols], base_r.at[me], sem_base.at[me]

        src, dst, sem = pair(me)
        pltpu.make_async_copy(src, dst, sem).start()
        for bits in PARTNERS:
            target = me ^ bits
            src, dst, sem = pair(target)
            pltpu.make_async_remote_copy(
                src_ref=src, dst_ref=dst, send_sem=sem_ds.at[kind], recv_sem=sem,
                device_id=(target, dp), device_id_type=MESH,
            ).start()

    def wts_on(n, k):
        s = 2 * n + z % 2
        part = pl.ds(k * UNITS, UNITS)
        return pltpu.make_async_remote_copy(
            src_ref=wts_r.at[s, part], dst_ref=wts_r.at[s, part], send_sem=sem_fw.at[n],
            recv_sem=sem_wts.at[s], device_id=(me, mates[k]), device_id_type=MESH,
        )

    def pass_on(n, _):
        s = 2 * n + z % 2
        held(wts_r.at[s], sem_wts.at[s])
        for k in range(2):
            wts_on(n, k).start()
        return 0

    direct = core == z % 2

    @pl.when(direct)
    def _():
        data_send(0)

    data_send(1)
    data_send(2)
    lax.fori_loop(0, NSEC // 2, pass_on, 0)

    block = lax.broadcasted_iota(jnp.int32, (128, CH), 0)
    feature = lax.broadcasted_iota(jnp.int32, (128, CH), 1)
    spread[...] = jnp.where((block & 31) == (feature >> 7), 1.0, 0.0).astype(BF16)
    pay[...] = jnp.zeros(pay.shape, F32)
    bpad[...] = jnp.zeros(bpad.shape, F32)
    bef_all[...] = jnp.zeros(bef_all.shape, F32)

    for h in range(2):
        held(hid_r.at[h], sem_hr.at[h])
    first = join_parts(hid_r)
    a_ref[0] = first[0:HALF]
    a_ref[1] = first[HALF:ROWS]

    lane = lanes((HALF, 128))
    lane64 = lanes((16, 128))

    def prefetch(s):
        packed = fx_r[s, 0:16].astype(F32)
        small = jnp.concatenate(
            [jnp.where((lane64 >= 32 * g) & (lane64 < 32 * g + 9), packed, 0.0) for g in range(4)],
            axis=0,
        )
        inverse = jnp.where(small > 0.0, 1.0 / jnp.where(small > 0.0, small, 1.0), 0.0)
        factor_ref[...] = dot(small.astype(BF16), spread[...])
        scale_ref[...] = dot(inverse.astype(BF16), spread[...])

    def stat_copy(s, h, j):
        target = peer_segs[j]
        return pltpu.make_async_remote_copy(
            src_ref=stat_s.at[s, h], dst_ref=stat_r.at[s, h, j - 1], send_sem=sem_st_s.at[s, h],
            recv_sem=sem_st_r.at[s, h], device_id=(target, dp), device_id_type=MESH,
        )

    def start(s, h):
        if h == 0:
            held(base_r.at[s], sem_base.at[s])

        rows = slice(HALF * h, HALF * h + HALF)
        total = jnp.zeros((HALF, 128), F32)
        for i in range(CH // 128):
            cols = slice(128 * i, 128 * i + 128)
            base = base_r[s, 2 * h : 2 * h + 2, :, cols].reshape(HALF, 128).astype(F32)
            coded = ((a_ref[h, :, cols] - base) * scale_ref[rows, cols]).astype(BF16)
            decoded = base + jnp.clip(coded.astype(F32), -448.0, 448.0) * factor_ref[rows, cols]
            d_ref[s % 2, h, :, cols] = decoded
            total = total + decoded
        own_mean = jnp.sum(total, axis=1, keepdims=True) * (1.0 / CH)
        squares = jnp.zeros((HALF, 128), F32)
        for i in range(CH // 128):
            cols = slice(128 * i, 128 * i + 128)
            center = d_ref[s % 2, h, :, cols] - own_mean
            squares = squares + center * center
            cen_ref[h, :, cols] = center.astype(BF16)
        own_m2 = jnp.sum(squares, axis=1, keepdims=True)
        pay[h, :, 0:UNITS] = dot(cen_ref[h], wts_r[s, 0:UNITS, :], NT)
        row = jnp.where(lane == 16 + chunk, own_mean, pay[h])
        row = jnp.where(lane == 24, own_m2, row)
        packed = row[0:8]
        for g in range(1, 4):
            packed = packed + pltpu.roll(row[8 * g : 8 * g + 8], 32 * g, 1)
        stat_s[s, h] = packed
        for j in range(1, NCH):
            stat_copy(s, h, j).start()

    def finish(s, h):
        up = wts_r[s, UNITS : 2 * UNITS, :]
        held(stat_r.at[s, h], sem_st_r.at[s, h])
        total = stat_s[s, h]
        for j in range(NCH - 1):
            total = total + stat_r[s, h, j]
        rows = jnp.concatenate(
            [total] + [pltpu.roll(total, 128 - 32 * g, 1) for g in range(1, 4)], axis=0
        )
        is_mean = (lane >= 16) & (lane < 24)
        mean = jnp.sum(jnp.where(is_mean, rows, 0.0), axis=1, keepdims=True) * (1.0 / NCH)
        off = jnp.where(is_mean, rows - mean, 0.0)
        squares = jnp.sum(
            jnp.where(lane == 24, rows, 0.0) + CH * off * off, axis=1, keepdims=True
        )
        rstd = lax.rsqrt(squares * (1.0 / WIDTH) + 1e-05)
        shift = dot(off.astype(BF16), fx_r[s, 16:32], NT)
        before = (rows[:, 0:UNITS] + shift) * rstd
        act = gelu(before).astype(BF16)
        added = dot(act, up)
        a_ref[h] = (d_ref[s % 2, h] + added).astype(BF16).astype(F32)
        here = slice(HALF * h, HALF * h + HALF)
        bef_ref[s, here] = before
        act_ref[s, here] = act
        mean_ref[s, here] = mean
        rstd_ref[s, here] = rstd

    def mix_copy(s, j):
        return pltpu.make_async_remote_copy(
            src_ref=mix_s.at[s, pl.ds(pl.multiple_of(8 * peer_chunks[j], 8), 8)],
            dst_ref=mix_r.at[s, j - 1], send_sem=sem_mx_s.at[s], recv_sem=sem_mx_r.at[s],
            device_id=(peer_segs[j], dp), device_id_type=MESH,
        )

    def side_work(s):
        decoded = d_ref[s % 2].reshape(ROWS, CH)
        xhat = ((decoded - mean_ref[s]) * rstd_ref[s]).astype(BF16)
        xhat_ref[s] = xhat
        mix_s[s] = dot(xhat, wuc_all[...], NT)
        for j in range(1, NCH):
            mix_copy(s, j).start()
        bpad[:, 0:UNITS] = bef_ref[s]
        bef_all[s // 8] = bef_all[s // 8] + pltpu.roll(bpad[...], 16 * (s % 8), 1)

    def weights(s, _):
        held(fx_r.at[s], sem_fx.at[s])

        @pl.when(s % 2 != z % 2)
        def _():
            held(wts_r.at[s], sem_wts.at[s])

        up = wts_r[s, UNITS : 2 * UNITS, :]
        own = pl.ds(pl.multiple_of(s * UNITS, UNITS), UNITS)
        wu_all[own, :] = up
        wuc_all[own, :] = (up.astype(F32) - fx_r[s, 16:32, 1:2].astype(F32)).astype(BF16)
        wdc_all[s] = (
            wts_r[s, 0:UNITS, :].astype(F32) - fx_r[s, 16:32, 0:1].astype(F32)
        ).astype(BF16)
        return 0

    lax.fori_loop(0, NSEC, weights, 0)

    def cw_copy(j):
        return pltpu.make_async_remote_copy(
            src_ref=cw_s.at[pl.ds(pl.multiple_of(8 * peer_chunks[j], 8), 8)],
            dst_ref=cw_r.at[j - 1],
            send_sem=sem_cw_s.at[0], recv_sem=sem_cw_r.at[0],
            device_id=(peer_segs[j], dp), device_id_type=MESH,
        )

    def cotangent_products():
        for h in range(2):
            held(cot_r.at[h], sem_cr.at[h])
        cot = join_parts(cot_r)
        g_ref[...] = cot
        cw_s[...] = dot(cot.astype(BF16), wu_all[...], NT)
        for j in range(1, NCH):
            cw_copy(j).start()

    own_gram = pl.ds(pl.multiple_of(32 * chunk, 32), 32)

    def gram_copy(j):
        return pltpu.make_async_remote_copy(
            src_ref=gram_s.at[pl.ds(pl.multiple_of(32 * peer_chunks[j], 32), 32)],
            dst_ref=gram_r.at[j - 1],
            send_sem=sem_gr_s.at[0], recv_sem=sem_gr_r.at[0],
            device_id=(peer_segs[j], dp), device_id_type=MESH,
        )

    def gm_copy(j):
        return pltpu.make_async_remote_copy(
            src_ref=gm_ref.at[own_gram], dst_ref=gm_ref.at[own_gram],
            send_sem=sem_gm_s.at[0], recv_sem=sem_gm_r.at[0],
            device_id=(peer_segs[j], dp), device_id_type=MESH,
        )

    def gram_products():
        products = dot(wdc_all[...].reshape(256, CH), wuc_all[...], NT)
        row_sec = lax.broadcasted_iota(jnp.int32, (256, 256), 0) >> 4
        col_sec = lanes((256, 256)) >> 4
        gram_s[...] = jnp.where(col_sec < row_sec, products, 0.0)
        for j in range(1, NCH):
            gram_copy(j).start()

    prefetch(0)
    for h in range(2):
        start(0, h)
    prefetch(1)

    def step(s, _):
        for h in range(2):
            finish(s, h)
            start(s + 1, h)
        side_work(s)

        @pl.when(s + 2 < NSEC)
        def _():
            prefetch(s + 2)

        @pl.when(s == 0)
        def _():
            for x_to in range(2):
                part_copy(x_to, cot_s, cot_r, sem_cs, sem_cr, True)

        @pl.when(s == 2)
        def _():
            cotangent_products()

        @pl.when(s == 3)
        def _():
            gram_products()

        @pl.when(s == 6)
        def _():
            held(gram_r, sem_gr_r.at[0])
            total = gram_s[own_gram, :]
            for j in range(NCH - 1):
                total = total + gram_r[j]
            gm_ref[own_gram, :] = total.astype(BF16)
            for j in range(1, NCH):
                gm_copy(j).start()

        return 0

    lax.fori_loop(0, NSEC - 1, step, 0)

    for h in range(2):
        finish(NSEC - 1, h)
    side_work(NSEC - 1)

    mine = pl.ds(pl.multiple_of(8 * chunk, 8), 8)

    def fold(t, _):
        held(mix_r.at[t], sem_mx_r.at[t])
        both = mix_s[t, mine, :]
        for j in range(NCH - 1):
            both = both + mix_r[t, j]
        xt_ref[t] = jnp.where(lanes((8, 256)) < UNITS * t, both, 0.0)
        return 0

    held(gm_ref.at[0 : 256 - 32], sem_gm_r.at[0])
    held(cw_r, sem_cw_r.at[0])
    grad_act = cw_s[mine, :]
    for j in range(NCH - 1):
        grad_act = grad_act + cw_r[j]
    bef8 = jnp.concatenate([bef_all[0, mine, :], bef_all[1, mine, :]], axis=1)
    slope8 = gelu_slope(bef8)
    lane8 = lanes((8, 256))
    lax.fori_loop(0, NSEC, fold, 0)

    def back(i, carry):
        grad_act, out = carry
        t = NSEC - 1 - i
        here = (lane8 >= UNITS * t) & (lane8 < UNITS * t + UNITS)
        grad_bef = jnp.where(here, grad_act * slope8, 0.0).astype(BF16)
        wide = grad_bef.astype(F32)
        c2 = jnp.sum(wide * bef8, axis=1, keepdims=True) * (1.0 / WIDTH)
        change = dot(grad_bef, gm_ref[...]) - c2 * xt_ref[t]
        return grad_act + rstd_ref[t, mine, :] * change, out + wide

    _, grad_bef = lax.fori_loop(0, NSEC, back, (grad_act, jnp.zeros((8, 256), F32)))
    gb_s[0] = grad_bef[:, 0:128]
    gb_s[1] = grad_bef[:, 128:256]

    def gb_copy(j):
        target = peer_segs[j]
        return pltpu.make_async_remote_copy(
            src_ref=gb_s, dst_ref=gb_r.at[:, mine], send_sem=sem_gb_s.at[0],
            recv_sem=sem_gb_r.at[0], device_id=(target, dp), device_id_type=MESH,
        )

    for j in range(1, NCH):
        gb_copy(j).start()
    gb_r[0, mine, :] = grad_bef[:, 0:128]
    gb_r[1, mine, :] = grad_bef[:, 128:256]
    held(gb_r.at[:, 0 : ROWS - 8], sem_gb_r.at[0])

    def x_copy(t, kind):
        to, at = (t // 2) % 2, 2 * (t // 4) + t % 2
        a, b = lax.rem(to + xh, 2), lax.rem(kind + xl, 2)
        slot = jnp.maximum(2 * a + b - 1, 0)
        return 2 * a + b, pltpu.make_async_remote_copy(
            src_ref=parts.at[to, kind, at], dst_ref=x_r.at[at, slot], send_sem=sem_xs.at[t, kind],
            recv_sem=sem_xr.at[at], device_id=(4 * y + 2 * to + core, 2 * z + kind),
            device_id_type=MESH,
        )

    def grads(i, _):
        t = NSEC - 1 - i
        to, at = (t // 2) % 2, 2 * (t // 4) + t % 2
        turned = pltpu.roll(gb_r[t // 8], lax.rem(128 - 16 * (t % 8), 128), 1)[:, 0:UNITS]
        grad_bef = turned.astype(BF16)
        g = g_ref[...]
        xhat = xhat_ref[t]
        parts[to, 0, at] = dot(grad_bef, xhat, TN).astype(BF16)
        parts[to, 1, at] = dot(act_ref[t], g.astype(BF16), TN).astype(BF16)
        for kind in range(2):
            away, copy = x_copy(t, kind)

            @pl.when(away > 0)
            def _():
                copy.start()

        c2 = jnp.sum(turned * bef_ref[t], axis=1, keepdims=True) * (1.0 / WIDTH)
        g_ref[...] = g + rstd_ref[t] * (dot(grad_bef, wdc_all[t]) - xhat.astype(F32) * c2)
        return 0

    lax.fori_loop(0, NSEC, grads, 0)

    def z_copy(i, h):
        to = lax.rem(i + 4 * core, NCH) + NCH * h
        ahead = lax.rem(to - z + NZ, NZ)
        return to, pltpu.make_async_remote_copy(
            src_ref=z_s.at[i, :, SPLIT[h]], dst_ref=z_r.at[ahead, :, 0 : SIZES[h]],
            send_sem=sem_zs.at[to], recv_sem=sem_zr.at[0],
            device_id=(me, 2 * to + xl), device_id_type=MESH,
        )

    def z_send(n, _):
        i = NCH - 1 - n
        total = parts[xh, xl, i].astype(F32)
        held(x_r.at[i], sem_xr.at[i])
        for k in range(3):
            total = total + x_r[i, k].astype(F32)
        z_s[i] = total.astype(BF16)
        for h in range(2):
            to, copy = z_copy(i, h)

            @pl.when(to != z)
            def _():
                copy.start()

        return 0

    lax.fori_loop(0, NCH, z_send, 0)
    f_total = jnp.concatenate(
        [z_s[pick, :, pl.ds(pl.multiple_of(640 * half, 128), 512)], z_s[pick, :, 512:640]],
        axis=1,
    ).astype(F32)
    for h in range(2):

        @pl.when(half == h)
        def _():
            held(z_r.at[1:NZ, :, 0 : SIZES[h]], sem_zr.at[0])

    f_s[...] = lax.fori_loop(
        1, NZ, lambda n, total: total + z_r[n].astype(F32), f_total
    ).astype(BF16)

    def a_copy(to, h):
        return pltpu.make_async_remote_copy(
            src_ref=f_s.at[:, 0 : SIZES[h]], dst_ref=a_r.at[chunk, h, :, 0 : SIZES[h]],
            send_sem=sem_as.at[to], recv_sem=sem_ar.at[chunk, h],
            device_id=(goal, 2 * to + xl), device_id_type=MESH,
        )

    def a_send(j, _):
        ahead = jnp.where(j % 2 == 1, (j + 1) // 2, NZ - j // 2)
        to = lax.rem(z + ahead, NZ)
        here = (goal == me) & (to == z)
        for h in range(2):

            @pl.when(jnp.logical_not(here) & (half == h))
            def _():
                a_copy(to, h).start()

            @pl.when(here & (half == h))
            def _():
                pltpu.make_async_copy(
                    f_s.at[:, 0 : SIZES[h]], a_r.at[chunk, h, :, 0 : SIZES[h]],
                    sem_ar.at[chunk, h],
                ).start()

        return 0

    lax.fori_loop(0, NZ, lambda n, _: a_send(NZ - 1 - n, 0), 0)

    def b_copy(q, h):
        return pltpu.make_async_remote_copy(
            src_ref=a_r.at[q, h, :, 0 : SIZES[h]], dst_ref=b_r.at[q, h, :, 0 : SIZES[h]],
            send_sem=sem_bs.at[q, h],
            recv_sem=sem_br.at[q, h], device_id=(me, 2 * z + 1 - xl), device_id_type=MESH,
        )

    for q in range(NCH):
        for h in range(2):
            held(a_r.at[q, h, :, 0 : SIZES[h]], sem_ar.at[q, h])
            b_copy(q, h).start()

    for x_to in range(2):
        part_copy(x_to, hid_s, hid_r, sem_hs, sem_hr, False)
        part_copy(x_to, cot_s, cot_r, sem_cs, sem_cr, False)

    @pl.when(direct)
    def _():
        held(wts_r.at[0 : NSEC - 1], sem_ds.at[0])

    held(fx_r.at[0 : NSEC - 1], sem_ds.at[1])
    held(base_r.at[0 : NSEC - 1], sem_ds.at[2])

    def forwarded(n, _):
        held(wts_r.at[0], sem_fw.at[n])
        return 0

    lax.fori_loop(0, NSEC // 2, forwarded, 0)

    def left(s, _):
        for h in range(2):
            held(stat_r.at[s, h], sem_st_s.at[s, h])
        held(mix_r.at[s], sem_mx_s.at[s])
        for kind in range(2):
            away, copy = x_copy(s, kind)

            @pl.when(away > 0)
            def _():
                copy.wait_send()

        return 0

    lax.fori_loop(0, NSEC, left, 0)
    held(cw_r, sem_cw_s.at[0])
    held(gram_r, sem_gr_s.at[0])
    held(gm_ref.at[0 : 256 - 32], sem_gm_s.at[0])
    held(gb_r.at[:, 0 : ROWS - 8], sem_gb_s.at[0])

    def z_left(i, _):
        for h in range(2):
            to, copy = z_copy(i, h)

            @pl.when(to != z)
            def _():
                copy.wait_send()

        return 0

    lax.fori_loop(0, NCH, z_left, 0)

    def a_left(to, _):
        for h in range(2):

            @pl.when(((goal != me) | (to != z)) & (half == h))
            def _():
                a_copy(to, h).wait_send()

        return 0

    lax.fori_loop(0, NZ, a_left, 0)

    for q in range(NCH):
        for h in range(2):
            b_copy(q, h).wait_recv()
            cols = slice(CH * q + SPLIT[h].start, CH * q + SPLIT[h].stop)
            own, other = a_r[q, h, :, 0 : SIZES[h]], b_r[q, h, :, 0 : SIZES[h]]
            down = jnp.where(xl == 0, own, other)
            up_ref[:, cols] = jnp.where(xl == 0, other, own)
            down_ref[:, cols] = (down.astype(F32) * gains_ref[:, cols].astype(F32)).astype(BF16)
    for q in range(NCH):
        for h in range(2):
            b_copy(q, h).wait_send()


def whole_call(ids, hid, cot, store, exps, gains, wd, wu):
    vmem = pl.BlockSpec(memory_space=pltpu.VMEM)
    dma = pltpu.SemaphoreType.DMA

    def bf(*shape):
        return pltpu.VMEM(shape, BF16)

    def f32(*shape):
        return pltpu.VMEM(shape, F32)

    out = jax.ShapeDtypeStruct((UNITS, WIDTH), BF16)
    peers = NCH - 1
    return pl.pallas_call(
        kernel,
        name="sections",
        out_shape=(out, out),
        in_specs=[pl.BlockSpec(memory_space=pltpu.SMEM), vmem, vmem,
                  pl.BlockSpec(memory_space=pl.ANY), vmem, vmem, vmem, vmem],
        out_specs=(vmem, vmem),
        scratch_shapes=[
            bf(8, 16, 640), bf(8, 16, 640), bf(2 * UNITS, WIDTH), bf(2, NCH, 32, 128),
            bf(2, 4, 16, 640), bf(2, 4, 16, 640), bf(NSEC, 2 * UNITS, CH), bf(NSEC, 32, 128),
            bf(NSEC, 4, 16, CH),
            bf(128, CH), f32(ROWS, CH), f32(ROWS, CH), bf(256, CH), bf(256, CH),
            bf(NSEC, UNITS, CH), f32(2, HALF, CH), f32(ROWS, CH), f32(2, 2, HALF, CH),
            bf(2, HALF, CH),
            f32(2, HALF, 128), f32(ROWS, 128), f32(2, ROWS, 128), f32(NSEC, ROWS, UNITS),
            bf(NSEC, ROWS, UNITS), f32(NSEC, ROWS, 1), f32(NSEC, ROWS, 1), bf(NSEC, ROWS, CH),
            f32(NSEC, 2, 8, 128), f32(NSEC, 2, peers, 8, 128),
            f32(NSEC, ROWS, 256), f32(NSEC, peers, 8, 256),
            f32(ROWS, 256), f32(peers, 8, 256), f32(256, 256), f32(peers, 32, 256), bf(256, 256), f32(NSEC, 8, 256),
            f32(2, 8, 128), f32(2, ROWS, 128),
            bf(2, 2, NCH, UNITS, CH), bf(NCH, 3, UNITS, CH), bf(NCH, UNITS, CH),
            bf(NZ, UNITS, 640), bf(UNITS, 640), bf(NCH, 2, UNITS, 640), bf(NCH, 2, UNITS, 640),
            dma((2,)), dma((2,)), dma((2,)), dma((2,)), dma((3,)), dma((NSEC,)), dma((NSEC,)),
            dma((NSEC,)), dma((NSEC // 2,)),
            dma((NSEC, 2)), dma((NSEC, 2)), dma((NSEC,)), dma((NSEC,)), dma((1,)), dma((1,)),
            dma((1,)), dma((1,)), dma((1,)), dma((1,)), dma((1,)), dma((1,)),
            dma((NSEC, 2)), dma((NCH,)), dma((NZ,)), dma((1,)), dma((NZ,)), dma((NCH, 2)),
            dma((NCH, 2)), dma((NCH, 2)),
        ],
        compiler_params=pltpu.CompilerParams(
            collective_id=1, has_side_effects=True, vmem_limit_bytes=56 * 2**20
        ),
    )(ids, hid, cot, store, exps, gains, wd, wu)


def shards(hidden_in, cotangent, stored_bases, sample_ids, block_exps, ln_gains, w_down, w_up):
    down, up = whole_call(
        sample_ids, hidden_in, cotangent, stored_bases[0], block_exps[0], ln_gains,
        jnp.swapaxes(w_down[0], 0, 1), w_up[0],
    )
    return jnp.swapaxes(down, 0, 1)[None], up[None]


def solution(mesh):
    return jax.shard_map(
        shards,
        mesh=mesh,
        in_specs=(
            P(None, "dp", "segment"),
            P(None, "dp", "segment"),
            P("segment", None, "dp", None),
            P("dp", None),
            P("segment", None, "dp", None),
            P("segment", None),
            P("segment", None, None),
            P("segment", None, None),
        ),
        out_specs=(P("segment", None, None), P("segment", None, None)),
        check_vma=False,
    )
```

```python
import functools

import jax
import jax.numpy as jnp
from jax import lax
from jax.experimental import pallas as pl
from jax.experimental.pallas import tpu as pltpu
from jax.sharding import PartitionSpec as P

MESH = pl.DeviceIdType.MESH
F32 = jnp.float32
BF16 = jnp.bfloat16
NSEC = 16
UNITS = 16
NCH = 8
CH = 1152
WIDTH = NCH * CH
SPLIT = (slice(0, 640), slice(640, 1152))
SIZES = (640, 512)
PEERS = ((0, 0), (2, 0), (2, 1), (1, 0), (3, 0), (1, 1), (3, 1), (0, 1))
PARTNERS = (2, 4, 12, 10, 6, 14, 8, 3, 5, 13, 11, 7, 15, 9, 1)
PART = 576
NZ = 16
ROWS = 64
HALF = 32
NT = (((1,), (1,)), ((), ()))
TN = (((0,), (0,)), ((), ()))
K_GELU = 0.7978845608028654
C_GELU = 0.044715


def dot(a, b, dims=(((1,), (0,)), ((), ()))):
    return lax.dot_general(a, b, dims, preferred_element_type=F32)


def lanes(shape):
    return lax.broadcasted_iota(jnp.int32, shape, len(shape) - 1)


def gelu(x):
    return 0.5 * x * (1.0 + jnp.tanh(K_GELU * (x + C_GELU * x * x * x)))


def gelu_slope(x):
    th = jnp.tanh(K_GELU * (x + C_GELU * x * x * x))
    return 0.5 * (1.0 + th) + 0.5 * x * (1.0 - th * th) * K_GELU * (1.0 + 3.0 * C_GELU * x * x)


def power_of_two(exps):
    factor = jnp.ones(exps.shape, F32)
    for bit in range(5):
        factor = jnp.where(((-exps) >> bit) & 1 == 1, factor * F32(0.5 ** (1 << bit)), factor)
    return factor


def join_parts(ref):
    first = ref[0].reshape(ROWS, 640).astype(F32)
    second = ref[1].reshape(ROWS, 640).astype(F32)
    lane = lanes((ROWS, 128))
    turned = [pltpu.roll(second[:, 128 * i : 128 * i + 128], 64, 1) for i in range(5)]
    tiles = [first[:, 128 * i : 128 * i + 128] for i in range(4)]
    tiles.append(jnp.where(lane < 64, first[:, 512:640], turned[0]))
    for i in range(4):
        tiles.append(jnp.where(lane < 64, turned[i], turned[i + 1]))
    return jnp.concatenate(tiles, axis=1)


def held(ref, sem):
    pltpu.make_async_copy(ref, ref, sem).wait()


def kernel(
    ids_ref, hid_ref, cot_ref, store_ref, exps_ref, gains_ref, wd_ref, wu_ref,
    down_ref, up_ref,
    hid_s, cot_s, wts_s, fx_s, hid_r, cot_r, wts_r, fx_r, base_r,
    spread, factor_ref, scale_ref, wu_all, wuc_all, wdc_all, a_ref, g_ref, d_ref, cen_ref,
    pay, bpad, bef_all, bef_ref, act_ref, mean_ref, rstd_ref, xhat_ref,
    stat_s, stat_r, mix_s, mix_r, cw_s, cw_r, gram_s, gram_r, gm_ref, xt_ref, gb_s, gb_r,
    parts, x_r, z_s, z_r, f_s, a_r, b_r,
    sem_hs, sem_hr, sem_cs, sem_cr, sem_ds, sem_fx, sem_wts, sem_base, sem_fw,
    sem_st_s, sem_st_r, sem_mx_s, sem_mx_r, sem_cw_s, sem_cw_r, sem_gr_s, sem_gr_r,
    sem_gm_s, sem_gm_r, sem_gb_s, sem_gb_r,
    sem_xs, sem_xr, sem_zs, sem_zr, sem_as, sem_ar, sem_bs, sem_br,
):
    me = lax.axis_index("segment")
    dp = lax.axis_index("dp")
    y, xh, core = me // 4, (me // 2) % 2, me % 2
    z, xl = dp // 2, dp % 2
    chunk = 2 * y + core

    def seg_of(q):
        return 4 * (q // 2) + 2 * xh + q % 2

    peer_chunks = [2 * lax.rem(y + dy, 4) + lax.rem(core + dc, 2) for dy, dc in PEERS]
    peer_segs = [seg_of(q) for q in peer_chunks]
    pick, half = lax.rem(z % NCH + 4 * core, NCH), z // NCH
    goal = seg_of(pick)
    mates = [2 * lax.rem(z + step, NZ) + xl for step in (NZ - 1, 1)]

    barrier = pltpu.get_barrier_semaphore()

    def greet(device):
        pl.semaphore_signal(barrier, inc=1, device_id=device, device_id_type=MESH)

    def greet_lines(j, _):
        greet((lax.rem(me + j, NSEC), dp))
        greet((me, 2 * lax.rem(z + j, NZ) + xl))
        return 0

    lax.fori_loop(1, NSEC, greet_lines, 0)

    def x_device(a, b):
        return (4 * y + 2 * lax.rem(xh + a, 2) + core, 2 * z + lax.rem(xl + b, 2))

    for a, b in ((0, 1), (1, 0), (1, 1)):
        greet(x_device(a, b))

    def greet_goal(j, _):
        @pl.when((goal != me) | (j != z))
        def _():
            greet((goal, 2 * j + xl))

        source, at = seg_of(j // 2), lax.rem(chunk + 4 * ((j // 2) % 2), NCH) + NCH * (j % 2)

        @pl.when((source != me) | (at != z))
        def _():
            greet((source, 2 * at + xl))

        return 0

    lax.fori_loop(0, NZ, greet_goal, 0)

    hid_s[...] = jnp.zeros(hid_s.shape, BF16)
    cot_s[...] = jnp.zeros(cot_s.shape, BF16)
    lane16 = lanes((UNITS, 128))
    batches = []
    for slot in range(8):
        batch = jnp.int32(0)
        for k in range(8):
            batch = jnp.maximum(batch, jnp.where(ids_ref[0, k] == slot, k, 0))
        batches.append(batch)
        hid_s[slot, :, 0:PART] = hid_ref[batch]
        cot_s[slot, :, 0:PART] = cot_ref[batch]
    aux = jnp.zeros((UNITS, 128), F32)
    up_total = jnp.zeros((UNITS, 1), F32)
    down_total = jnp.zeros((UNITS, 1), F32)
    for q in range(NCH):
        part = slice(q * CH, (q + 1) * CH)
        scaled = (wd_ref[:, part].astype(F32) * gains_ref[:, part].astype(F32)).astype(BF16)
        wts_s[0:UNITS, part] = scaled
        up = wu_ref[:, part]
        wts_s[UNITS : 2 * UNITS, part] = up
        down_sum = jnp.sum(scaled.astype(F32), axis=1, keepdims=True)
        aux = aux + jnp.where(lane16 == 16 + q, down_sum, 0.0)
        down_total = down_total + down_sum
        up_total = up_total + jnp.sum(up.astype(F32), axis=1, keepdims=True)
    aux = aux + jnp.where(lane16 == 0, down_total * (1.0 / WIDTH), 0.0)
    aux = (aux + jnp.where(lane16 == 1, up_total * (1.0 / WIDTH), 0.0)).astype(BF16)
    bpad[...] = jnp.zeros(bpad.shape, F32)
    for x_to in range(2):
        picks = []
        for g in range(4):
            bpad[0:16, 0:72] = power_of_two(exps_ref[batches[4 * x_to + g]])
            picks.append(bpad[0:16, :])
        for q in range(NCH):
            packed = jnp.zeros((16, 128), F32)
            for g in range(4):
                turned = pltpu.roll(picks[g], (32 * g - 9 * q) % 128, 1)
                packed = jnp.where((lane16 >= 32 * g) & (lane16 < 32 * g + 9), turned, packed)
            fx_s[x_to, q, 0:16] = packed.astype(BF16)
            fx_s[x_to, q, 16:32] = aux

    pl.semaphore_wait(
        barrier, 2 * (NSEC - 1) + 3 + 2 * NZ - 2 * jnp.where(goal == me, 1, 0)
    )

    def part_copy(x_to, src, dst, send, recv, go):
        target = 4 * y + 2 * x_to + xh
        rows = src.at[4 * x_to : 4 * x_to + 4]

        if go:

            @pl.when(target == me)
            def _():
                pltpu.make_async_copy(rows, dst.at[core], recv.at[core]).start()

        @pl.when(target != me)
        def _():
            copy = pltpu.make_async_remote_copy(
                src_ref=rows, dst_ref=dst.at[core], send_sem=send.at[x_to],
                recv_sem=recv.at[core], device_id=(target, dp), device_id_type=MESH,
            )
            copy.start() if go else copy.wait_send()

    for x_to in range(2):
        part_copy(x_to, hid_s, hid_r, sem_hs, sem_hr, True)

    def place(target):
        to_chunk = 2 * (target // 4) + target % 2
        return (target // 2) % 2, to_chunk, pl.ds(pl.multiple_of(to_chunk * CH, 128), CH)

    def data_send(kind):
        def pair(target):
            x_to, to_chunk, cols = place(target)
            if kind == 0:
                return wts_s.at[:, cols], wts_r.at[me], sem_wts.at[me]
            if kind == 1:
                return fx_s.at[x_to, to_chunk], fx_r.at[me], sem_fx.at[me]
            return store_ref.at[pl.ds(4 * x_to, 4), :, cols], base_r.at[me], sem_base.at[me]

        src, dst, sem = pair(me)
        pltpu.make_async_copy(src, dst, sem).start()
        for bits in PARTNERS:
            target = me ^ bits
            src, dst, sem = pair(target)
            pltpu.make_async_remote_copy(
                src_ref=src, dst_ref=dst, send_sem=sem_ds.at[kind], recv_sem=sem,
                device_id=(target, dp), device_id_type=MESH,
            ).start()

    def wts_on(n, k):
        s = 2 * n + z % 2
        part = pl.ds(k * UNITS, UNITS)
        return pltpu.make_async_remote_copy(
            src_ref=wts_r.at[s, part], dst_ref=wts_r.at[s, part], send_sem=sem_fw.at[n],
            recv_sem=sem_wts.at[s], device_id=(me, mates[k]), device_id_type=MESH,
        )

    def pass_on(n, _):
        s = 2 * n + z % 2
        held(wts_r.at[s], sem_wts.at[s])
        for k in range(2):
            wts_on(n, k).start()
        return 0

    direct = core == z % 2

    @pl.when(direct)
    def _():
        data_send(0)

    data_send(1)
    data_send(2)
    lax.fori_loop(0, NSEC // 2, pass_on, 0)

    block = lax.broadcasted_iota(jnp.int32, (128, CH), 0)
    feature = lax.broadcasted_iota(jnp.int32, (128, CH), 1)
    spread[...] = jnp.where((block & 31) == (feature >> 7), 1.0, 0.0).astype(BF16)
    pay[...] = jnp.zeros(pay.shape, F32)
    bpad[...] = jnp.zeros(bpad.shape, F32)
    bef_all[...] = jnp.zeros(bef_all.shape, F32)

    for h in range(2):
        held(hid_r.at[h], sem_hr.at[h])
    first = join_parts(hid_r)
    a_ref[0] = first[0:HALF]
    a_ref[1] = first[HALF:ROWS]

    lane = lanes((HALF, 128))
    lane64 = lanes((16, 128))

    def prefetch(s):
        packed = fx_r[s, 0:16].astype(F32)
        small = jnp.concatenate(
            [jnp.where((lane64 >= 32 * g) & (lane64 < 32 * g + 9), packed, 0.0) for g in range(4)],
            axis=0,
        )
        inverse = jnp.where(small > 0.0, 1.0 / jnp.where(small > 0.0, small, 1.0), 0.0)
        factor_ref[...] = dot(small.astype(BF16), spread[...])
        scale_ref[...] = dot(inverse.astype(BF16), spread[...])

    def stat_copy(s, h, j):
        target = peer_segs[j]
        return pltpu.make_async_remote_copy(
            src_ref=stat_s.at[s, h], dst_ref=stat_r.at[s, h, j - 1], send_sem=sem_st_s.at[s, h],
            recv_sem=sem_st_r.at[s, h], device_id=(target, dp), device_id_type=MESH,
        )

    def start(s, h):
        if h == 0:
            held(base_r.at[s], sem_base.at[s])

        rows = slice(HALF * h, HALF * h + HALF)
        total = jnp.zeros((HALF, 128), F32)
        for i in range(CH // 128):
            cols = slice(128 * i, 128 * i + 128)
            base = base_r[s, 2 * h : 2 * h + 2, :, cols].reshape(HALF, 128).astype(F32)
            coded = ((a_ref[h, :, cols] - base) * scale_ref[rows, cols]).astype(BF16)
            decoded = base + jnp.clip(coded.astype(F32), -448.0, 448.0) * factor_ref[rows, cols]
            d_ref[s % 2, h, :, cols] = decoded
            total = total + decoded
        own_mean = jnp.sum(total, axis=1, keepdims=True) * (1.0 / CH)
        squares = jnp.zeros((HALF, 128), F32)
        for i in range(CH // 128):
            cols = slice(128 * i, 128 * i + 128)
            center = d_ref[s % 2, h, :, cols] - own_mean
            squares = squares + center * center
            cen_ref[h, :, cols] = center.astype(BF16)
        own_m2 = jnp.sum(squares, axis=1, keepdims=True)
        pay[h, :, 0:UNITS] = dot(cen_ref[h], wts_r[s, 0:UNITS, :], NT)
        row = jnp.where(lane == 16 + chunk, own_mean, pay[h])
        row = jnp.where(lane == 24, own_m2, row)
        packed = row[0:8]
        for g in range(1, 4):
            packed = packed + pltpu.roll(row[8 * g : 8 * g + 8], 32 * g, 1)
        stat_s[s, h] = packed
        for j in range(1, NCH):
            stat_copy(s, h, j).start()

    def finish(s, h):
        up = wts_r[s, UNITS : 2 * UNITS, :]
        held(stat_r.at[s, h], sem_st_r.at[s, h])
        total = stat_s[s, h]
        for j in range(NCH - 1):
            total = total + stat_r[s, h, j]
        rows = jnp.concatenate(
            [total] + [pltpu.roll(total, 128 - 32 * g, 1) for g in range(1, 4)], axis=0
        )
        is_mean = (lane >= 16) & (lane < 24)
        mean = jnp.sum(jnp.where(is_mean, rows, 0.0), axis=1, keepdims=True) * (1.0 / NCH)
        off = jnp.where(is_mean, rows - mean, 0.0)
        squares = jnp.sum(
            jnp.where(lane == 24, rows, 0.0) + CH * off * off, axis=1, keepdims=True
        )
        rstd = lax.rsqrt(squares * (1.0 / WIDTH) + 1e-05)
        shift = dot(off.astype(BF16), fx_r[s, 16:32], NT)
        before = (rows[:, 0:UNITS] + shift) * rstd
        act = gelu(before).astype(BF16)
        added = dot(act, up)
        a_ref[h] = (d_ref[s % 2, h] + added).astype(BF16).astype(F32)
        here = slice(HALF * h, HALF * h + HALF)
        bef_ref[s, here] = before
        act_ref[s, here] = act
        mean_ref[s, here] = mean
        rstd_ref[s, here] = rstd

    def mix_copy(s, j):
        return pltpu.make_async_remote_copy(
            src_ref=mix_s.at[s, pl.ds(pl.multiple_of(8 * peer_chunks[j], 8), 8)],
            dst_ref=mix_r.at[s, j - 1], send_sem=sem_mx_s.at[s], recv_sem=sem_mx_r.at[s],
            device_id=(peer_segs[j], dp), device_id_type=MESH,
        )

    def side_work(s):
        decoded = d_ref[s % 2].reshape(ROWS, CH)
        xhat = ((decoded - mean_ref[s]) * rstd_ref[s]).astype(BF16)
        xhat_ref[s] = xhat
        mix_s[s] = dot(xhat, wuc_all[...], NT)
        for j in range(1, NCH):
            mix_copy(s, j).start()
        bpad[:, 0:UNITS] = bef_ref[s]
        bef_all[s // 8] = bef_all[s // 8] + pltpu.roll(bpad[...], 16 * (s % 8), 1)

    def weights(s, _):
        held(fx_r.at[s], sem_fx.at[s])

        @pl.when(s % 2 != z % 2)
        def _():
            held(wts_r.at[s], sem_wts.at[s])

        up = wts_r[s, UNITS : 2 * UNITS, :]
        own = pl.ds(pl.multiple_of(s * UNITS, UNITS), UNITS)
        wu_all[own, :] = up
        wuc_all[own, :] = (up.astype(F32) - fx_r[s, 16:32, 1:2].astype(F32)).astype(BF16)
        wdc_all[s] = (
            wts_r[s, 0:UNITS, :].astype(F32) - fx_r[s, 16:32, 0:1].astype(F32)
        ).astype(BF16)
        return 0

    wuc_all[...] = jnp.zeros(wuc_all.shape, BF16)
    for s in range(2):
        weights(s, 0)

    def cw_copy(j):
        return pltpu.make_async_remote_copy(
            src_ref=cw_s.at[pl.ds(pl.multiple_of(8 * peer_chunks[j], 8), 8)],
            dst_ref=cw_r.at[j - 1],
            send_sem=sem_cw_s.at[0], recv_sem=sem_cw_r.at[0],
            device_id=(peer_segs[j], dp), device_id_type=MESH,
        )

    def cotangent_products():
        for h in range(2):
            held(cot_r.at[h], sem_cr.at[h])
        cot = join_parts(cot_r)
        g_ref[...] = cot
        cw_s[...] = dot(cot.astype(BF16), wu_all[...], NT)
        for j in range(1, NCH):
            cw_copy(j).start()

    own_gram = pl.ds(pl.multiple_of(32 * chunk, 32), 32)

    def gram_copy(j):
        return pltpu.make_async_remote_copy(
            src_ref=gram_s.at[pl.ds(pl.multiple_of(32 * peer_chunks[j], 32), 32)],
            dst_ref=gram_r.at[j - 1],
            send_sem=sem_gr_s.at[0], recv_sem=sem_gr_r.at[0],
            device_id=(peer_segs[j], dp), device_id_type=MESH,
        )

    def gm_copy(j):
        return pltpu.make_async_remote_copy(
            src_ref=gm_ref.at[own_gram], dst_ref=gm_ref.at[own_gram],
            send_sem=sem_gm_s.at[0], recv_sem=sem_gm_r.at[0],
            device_id=(peer_segs[j], dp), device_id_type=MESH,
        )

    def gram_products():
        products = dot(wdc_all[...].reshape(256, CH), wuc_all[...], NT)
        row_sec = lax.broadcasted_iota(jnp.int32, (256, 256), 0) >> 4
        col_sec = lanes((256, 256)) >> 4
        gram_s[...] = jnp.where(col_sec < row_sec, products, 0.0)
        for j in range(1, NCH):
            gram_copy(j).start()

    prefetch(0)
    for h in range(2):
        start(0, h)
    prefetch(1)

    def step(s, _):
        for h in range(2):
            finish(s, h)
            start(s + 1, h)
        side_work(s)
        for k in range(3):
            later = 2 + 3 * s + k

            @pl.when(later < NSEC)
            def _():
                weights(later, 0)

        @pl.when(s + 2 < NSEC)
        def _():
            prefetch(s + 2)

        @pl.when(s == 0)
        def _():
            for x_to in range(2):
                part_copy(x_to, cot_s, cot_r, sem_cs, sem_cr, True)

        @pl.when(s == 5)
        def _():
            cotangent_products()

        @pl.when(s == 6)
        def _():
            gram_products()

        @pl.when(s == 9)
        def _():
            held(gram_r, sem_gr_r.at[0])
            total = gram_s[own_gram, :]
            for j in range(NCH - 1):
                total = total + gram_r[j]
            gm_ref[own_gram, :] = total.astype(BF16)
            for j in range(1, NCH):
                gm_copy(j).start()

        return 0

    lax.fori_loop(0, NSEC - 1, step, 0)

    for h in range(2):
        finish(NSEC - 1, h)
    side_work(NSEC - 1)

    mine = pl.ds(pl.multiple_of(8 * chunk, 8), 8)

    def fold(t, _):
        held(mix_r.at[t], sem_mx_r.at[t])
        both = mix_s[t, mine, :]
        for j in range(NCH - 1):
            both = both + mix_r[t, j]
        xt_ref[t] = jnp.where(lanes((8, 256)) < UNITS * t, both, 0.0)
        return 0

    held(gm_ref.at[0 : 256 - 32], sem_gm_r.at[0])
    held(cw_r, sem_cw_r.at[0])
    grad_act = cw_s[mine, :]
    for j in range(NCH - 1):
        grad_act = grad_act + cw_r[j]
    bef8 = jnp.concatenate([bef_all[0, mine, :], bef_all[1, mine, :]], axis=1)
    slope8 = gelu_slope(bef8)
    lane8 = lanes((8, 256))
    lax.fori_loop(0, NSEC, fold, 0)

    def back(i, carry):
        grad_act, out = carry
        t = NSEC - 1 - i
        here = (lane8 >= UNITS * t) & (lane8 < UNITS * t + UNITS)
        grad_bef = jnp.where(here, grad_act * slope8, 0.0).astype(BF16)
        wide = grad_bef.astype(F32)
        c2 = jnp.sum(wide * bef8, axis=1, keepdims=True) * (1.0 / WIDTH)
        change = dot(grad_bef, gm_ref[...]) - c2 * xt_ref[t]
        return grad_act + rstd_ref[t, mine, :] * change, out + wide

    _, grad_bef = lax.fori_loop(0, NSEC, back, (grad_act, jnp.zeros((8, 256), F32)))
    gb_s[0] = grad_bef[:, 0:128]
    gb_s[1] = grad_bef[:, 128:256]

    def gb_copy(j):
        target = peer_segs[j]
        return pltpu.make_async_remote_copy(
            src_ref=gb_s, dst_ref=gb_r.at[:, mine], send_sem=sem_gb_s.at[0],
            recv_sem=sem_gb_r.at[0], device_id=(target, dp), device_id_type=MESH,
        )

    for j in range(1, NCH):
        gb_copy(j).start()
    gb_r[0, mine, :] = grad_bef[:, 0:128]
    gb_r[1, mine, :] = grad_bef[:, 128:256]
    held(gb_r.at[:, 0 : ROWS - 8], sem_gb_r.at[0])

    def x_copy(t, kind):
        to, at = (t // 2) % 2, 2 * (t // 4) + t % 2
        a, b = lax.rem(to + xh, 2), lax.rem(kind + xl, 2)
        slot = jnp.maximum(2 * a + b - 1, 0)
        return 2 * a + b, pltpu.make_async_remote_copy(
            src_ref=parts.at[to, kind, at], dst_ref=x_r.at[at, slot], send_sem=sem_xs.at[t, kind],
            recv_sem=sem_xr.at[at], device_id=(4 * y + 2 * to + core, 2 * z + kind),
            device_id_type=MESH,
        )

    def grads(i, _):
        t = NSEC - 1 - i
        to, at = (t // 2) % 2, 2 * (t // 4) + t % 2
        turned = pltpu.roll(gb_r[t // 8], lax.rem(128 - 16 * (t % 8), 128), 1)[:, 0:UNITS]
        grad_bef = turned.astype(BF16)
        g = g_ref[...]
        xhat = xhat_ref[t]
        parts[to, 0, at] = dot(grad_bef, xhat, TN).astype(BF16)
        parts[to, 1, at] = dot(act_ref[t], g.astype(BF16), TN).astype(BF16)
        for kind in range(2):
            away, copy = x_copy(t, kind)

            @pl.when(away > 0)
            def _():
                copy.start()

        c2 = jnp.sum(turned * bef_ref[t], axis=1, keepdims=True) * (1.0 / WIDTH)
        g_ref[...] = g + rstd_ref[t] * (dot(grad_bef, wdc_all[t]) - xhat.astype(F32) * c2)
        return 0

    lax.fori_loop(0, NSEC, grads, 0)

    def z_copy(i, h):
        to = lax.rem(i + 4 * core, NCH) + NCH * h
        ahead = lax.rem(to - z + NZ, NZ)
        return to, pltpu.make_async_remote_copy(
            src_ref=z_s.at[i, :, SPLIT[h]], dst_ref=z_r.at[ahead, :, 0 : SIZES[h]],
            send_sem=sem_zs.at[to], recv_sem=sem_zr.at[0],
            device_id=(me, 2 * to + xl), device_id_type=MESH,
        )

    def z_send(n, _):
        i = NCH - 1 - n
        total = parts[xh, xl, i].astype(F32)
        held(x_r.at[i], sem_xr.at[i])
        for k in range(3):
            total = total + x_r[i, k].astype(F32)
        z_s[i] = total.astype(BF16)
        for h in range(2):
            to, copy = z_copy(i, h)

            @pl.when(to != z)
            def _():
                copy.start()

        return 0

    lax.fori_loop(0, NCH, z_send, 0)
    f_total = jnp.concatenate(
        [z_s[pick, :, pl.ds(pl.multiple_of(640 * half, 128), 512)], z_s[pick, :, 512:640]],
        axis=1,
    ).astype(F32)
    for h in range(2):

        @pl.when(half == h)
        def _():
            held(z_r.at[1:NZ, :, 0 : SIZES[h]], sem_zr.at[0])

    f_s[...] = lax.fori_loop(
        1, NZ, lambda n, total: total + z_r[n].astype(F32), f_total
    ).astype(BF16)

    def a_copy(to, h):
        return pltpu.make_async_remote_copy(
            src_ref=f_s.at[:, 0 : SIZES[h]], dst_ref=a_r.at[chunk, h, :, 0 : SIZES[h]],
            send_sem=sem_as.at[to], recv_sem=sem_ar.at[chunk, h],
            device_id=(goal, 2 * to + xl), device_id_type=MESH,
        )

    def a_send(j, _):
        ahead = jnp.where(j % 2 == 1, (j + 1) // 2, NZ - j // 2)
        to = lax.rem(z + ahead, NZ)
        here = (goal == me) & (to == z)
        for h in range(2):

            @pl.when(jnp.logical_not(here) & (half == h))
            def _():
                a_copy(to, h).start()

            @pl.when(here & (half == h))
            def _():
                pltpu.make_async_copy(
                    f_s.at[:, 0 : SIZES[h]], a_r.at[chunk, h, :, 0 : SIZES[h]],
                    sem_ar.at[chunk, h],
                ).start()

        return 0

    lax.fori_loop(0, NZ, lambda n, _: a_send(NZ - 1 - n, 0), 0)

    def b_copy(q, h):
        return pltpu.make_async_remote_copy(
            src_ref=a_r.at[q, h, :, 0 : SIZES[h]], dst_ref=b_r.at[q, h, :, 0 : SIZES[h]],
            send_sem=sem_bs.at[q, h],
            recv_sem=sem_br.at[q, h], device_id=(me, 2 * z + 1 - xl), device_id_type=MESH,
        )

    for q in range(NCH):
        for h in range(2):
            held(a_r.at[q, h, :, 0 : SIZES[h]], sem_ar.at[q, h])
            b_copy(q, h).start()

    for x_to in range(2):
        part_copy(x_to, hid_s, hid_r, sem_hs, sem_hr, False)
        part_copy(x_to, cot_s, cot_r, sem_cs, sem_cr, False)

    @pl.when(direct)
    def _():
        held(wts_r.at[0 : NSEC - 1], sem_ds.at[0])

    held(fx_r.at[0 : NSEC - 1], sem_ds.at[1])
    held(base_r.at[0 : NSEC - 1], sem_ds.at[2])

    def forwarded(n, _):
        held(wts_r.at[0], sem_fw.at[n])
        return 0

    lax.fori_loop(0, NSEC // 2, forwarded, 0)

    def left(s, _):
        for h in range(2):
            held(stat_r.at[s, h], sem_st_s.at[s, h])
        held(mix_r.at[s], sem_mx_s.at[s])
        for kind in range(2):
            away, copy = x_copy(s, kind)

            @pl.when(away > 0)
            def _():
                copy.wait_send()

        return 0

    lax.fori_loop(0, NSEC, left, 0)
    held(cw_r, sem_cw_s.at[0])
    held(gram_r, sem_gr_s.at[0])
    held(gm_ref.at[0 : 256 - 32], sem_gm_s.at[0])
    held(gb_r.at[:, 0 : ROWS - 8], sem_gb_s.at[0])

    def z_left(i, _):
        for h in range(2):
            to, copy = z_copy(i, h)

            @pl.when(to != z)
            def _():
                copy.wait_send()

        return 0

    lax.fori_loop(0, NCH, z_left, 0)

    def a_left(to, _):
        for h in range(2):

            @pl.when(((goal != me) | (to != z)) & (half == h))
            def _():
                a_copy(to, h).wait_send()

        return 0

    lax.fori_loop(0, NZ, a_left, 0)

    for q in range(NCH):
        for h in range(2):
            b_copy(q, h).wait_recv()
            cols = slice(CH * q + SPLIT[h].start, CH * q + SPLIT[h].stop)
            own, other = a_r[q, h, :, 0 : SIZES[h]], b_r[q, h, :, 0 : SIZES[h]]
            down = jnp.where(xl == 0, own, other)
            up_ref[:, cols] = jnp.where(xl == 0, other, own)
            down_ref[:, cols] = (down.astype(F32) * gains_ref[:, cols].astype(F32)).astype(BF16)
    for q in range(NCH):
        for h in range(2):
            b_copy(q, h).wait_send()


def whole_call(ids, hid, cot, store, exps, gains, wd, wu):
    vmem = pl.BlockSpec(memory_space=pltpu.VMEM)
    dma = pltpu.SemaphoreType.DMA

    def bf(*shape):
        return pltpu.VMEM(shape, BF16)

    def f32(*shape):
        return pltpu.VMEM(shape, F32)

    out = jax.ShapeDtypeStruct((UNITS, WIDTH), BF16)
    peers = NCH - 1
    return pl.pallas_call(
        kernel,
        name="sections",
        out_shape=(out, out),
        in_specs=[pl.BlockSpec(memory_space=pltpu.SMEM), vmem, vmem,
                  pl.BlockSpec(memory_space=pl.ANY), vmem, vmem, vmem, vmem],
        out_specs=(vmem, vmem),
        scratch_shapes=[
            bf(8, 16, 640), bf(8, 16, 640), bf(2 * UNITS, WIDTH), bf(2, NCH, 32, 128),
            bf(2, 4, 16, 640), bf(2, 4, 16, 640), bf(NSEC, 2 * UNITS, CH), bf(NSEC, 32, 128),
            bf(NSEC, 4, 16, CH),
            bf(128, CH), f32(ROWS, CH), f32(ROWS, CH), bf(256, CH), bf(256, CH),
            bf(NSEC, UNITS, CH), f32(2, HALF, CH), f32(ROWS, CH), f32(2, 2, HALF, CH),
            bf(2, HALF, CH),
            f32(2, HALF, 128), f32(ROWS, 128), f32(2, ROWS, 128), f32(NSEC, ROWS, UNITS),
            bf(NSEC, ROWS, UNITS), f32(NSEC, ROWS, 1), f32(NSEC, ROWS, 1), bf(NSEC, ROWS, CH),
            f32(NSEC, 2, 8, 128), f32(NSEC, 2, peers, 8, 128),
            f32(NSEC, ROWS, 256), f32(NSEC, peers, 8, 256),
            f32(ROWS, 256), f32(peers, 8, 256), f32(256, 256), f32(peers, 32, 256), bf(256, 256), f32(NSEC, 8, 256),
            f32(2, 8, 128), f32(2, ROWS, 128),
            bf(2, 2, NCH, UNITS, CH), bf(NCH, 3, UNITS, CH), bf(NCH, UNITS, CH),
            bf(NZ, UNITS, 640), bf(UNITS, 640), bf(NCH, 2, UNITS, 640), bf(NCH, 2, UNITS, 640),
            dma((2,)), dma((2,)), dma((2,)), dma((2,)), dma((3,)), dma((NSEC,)), dma((NSEC,)),
            dma((NSEC,)), dma((NSEC // 2,)),
            dma((NSEC, 2)), dma((NSEC, 2)), dma((NSEC,)), dma((NSEC,)), dma((1,)), dma((1,)),
            dma((1,)), dma((1,)), dma((1,)), dma((1,)), dma((1,)), dma((1,)),
            dma((NSEC, 2)), dma((NCH,)), dma((NZ,)), dma((1,)), dma((NZ,)), dma((NCH, 2)),
            dma((NCH, 2)), dma((NCH, 2)),
        ],
        compiler_params=pltpu.CompilerParams(
            collective_id=1, has_side_effects=True, vmem_limit_bytes=56 * 2**20
        ),
    )(ids, hid, cot, store, exps, gains, wd, wu)


def shards(hidden_in, cotangent, stored_bases, sample_ids, block_exps, ln_gains, w_down, w_up):
    down, up = whole_call(
        sample_ids, hidden_in, cotangent, stored_bases[0], block_exps[0], ln_gains,
        jnp.swapaxes(w_down[0], 0, 1), w_up[0],
    )
    return jnp.swapaxes(down, 0, 1)[None], up[None]


def solution(mesh):
    return jax.shard_map(
        shards,
        mesh=mesh,
        in_specs=(
            P(None, "dp", "segment"),
            P(None, "dp", "segment"),
            P("segment", None, "dp", None),
            P("dp", None),
            P("segment", None, "dp", None),
            P("segment", None),
            P("segment", None, None),
            P("segment", None, None),
        ),
        out_specs=(P("segment", None, None), P("segment", None, None)),
        check_vma=False,
    )
```
